32 devices in a mesh: groups: 2 (over x), expert: 4 (over y, core), dp: 4 (over z).
Axes of the slice: x: 2, y: 2, z: 4, core: 2. Of those that a mesh axis runs over, the one named last changes fastest.
Arguments:
- tokens: bfloat16 [4096, 4096], P(('groups', 'expert', 'dp')), parts along dimension 0, may hold values from -6 to 6
- expert_ids: int32 [4096, 8], P(('groups', 'expert', 'dp')), parts along dimension 0, may hold values from 0 to 255, all different within a row; in each aligned block of 128 rows (0 to 127, 128 to 255, ...) at most 6 rows name the same one
- gate_codes: int32 [4096, 8], P(('groups', 'expert', 'dp')), parts along dimension 0, may hold values from 1 to 32767
- cotangent: bfloat16 [4096, 4096], P(('groups', 'expert', 'dp')), parts along dimension 0, may hold values from -6 to 6
- gate_weight: bfloat16 [4, 4096, 1024], P('expert', 'dp'), may hold values from -0.09375 to 0.09375
- up_weight: bfloat16 [4, 4096, 1024], P('expert', 'dp'), may hold values from -0.09375 to 0.09375
- down_weight: bfloat16 [4, 1024, 4096], P('expert', None, 'dp'), may hold values from -0.1875 to 0.1875
- first_moment: bfloat16 [8, 1024, 4096], P(('groups', 'expert'), None, 'dp'), parts along dimension 0, may hold values from -6 to 6
- second_moment: bfloat16 [8, 1024, 4096], P(('groups', 'expert'), None, 'dp'), parts along dimension 0, may hold values from 0.63671875 to 6.375
- selected: int32 [6], P('groups'), parts along dimension 0, may hold values from 0 to 3, as said below
Outputs:
- mixed: bfloat16 [4096, 4096], P(('groups', 'expert', 'dp')), parts along dimension 0
- input_grad: bfloat16 [4096, 4096], P(('groups', 'expert', 'dp')), parts along dimension 0
- adam_step: bfloat16 [8, 1024, 4096], P(('groups', 'expert'), None, 'dp'), parts along dimension 0
- new_first: bfloat16 [8, 1024, 4096], P(('groups', 'expert'), None, 'dp'), parts along dimension 0
- new_second: bfloat16 [8, 1024, 4096], P(('groups', 'expert'), None, 'dp'), parts along dimension 0
The draws below stay inside these ranges and needn't reach their ends.
There are 2 independent parts, one for each index of `groups`. The reference program is written for one: setup_inputs(seed, part) draws one part's arguments, and reference() takes and returns one part's arrays. A program takes and returns all parts, laid end to end along the dimension named above; an argument that names none is the same for every part. Nothing has to cross between parts.
Inputs may be any that keep to these rules, and one draw needn't show every extreme that they name: `expert_ids`: each row names 8 different experts; in each aligned block of 128 rows (the rows of one device) no expert is named by more than 6 rows. `selected`: 3 different expert ids.
All inputs are finite; a program needn't handle non-finite values.
Results may differ from the reference program's by a relative error of at most 0.0066.
Values may be sent and summed in bfloat16 or wider, within the bound.
No kernel may reach another device: no remote copies, remote signals or barrier semaphores. Data moves between devices by JAX's collectives and lax.ppermute only.
A program may use at most 64 MiB of HBM per device.

```python
import math
import jax
import jax.numpy as jnp
import numpy as np
from jax import lax

D = 4096
FF = 1024
ROUTED = 256
TOP = 8
TOK_DEV = 128
TOKENS = 2048
EXPERTS = 4
SEL = 3
CAP = 6
LIVE = 64


def draw_selected(key, part):
    key = jax.random.fold_in(key, 7)
    return jax.random.permutation(key, EXPERTS)[:SEL].astype(jnp.int32)


def set_ends(array, own_key, low, high):
    index_at = [jax.random.randint(jax.random.fold_in(own_key, axis), (), 0, length) for axis, length in enumerate(array.shape)]
    widest = array.shape.index(max(array.shape))
    beside = index_at[:widest] + [(index_at[widest] + 1) % array.shape[widest]] + index_at[widest + 1:]
    return array.at[tuple(index_at)].set(low).at[tuple(beside)].set(high)


def steps_of(own_key, dims, pieces, smallest, largest):
    loudness = 1.0
    for dim, parts in pieces:
        steps = jax.random.uniform(jax.random.fold_in(jax.random.fold_in(own_key, 6), dim), (parts,), jnp.float32, smallest / len(pieces), largest / len(pieces))
        loudness = loudness * jnp.repeat(jnp.exp(steps), dims[dim] // parts).reshape((-1,) + (1,) * (len(dims) - 1 - dim))
    return loudness


def assign_block(key, own, number, rows, count, top, bound, skew):
    sequence = jax.random.permutation(key, count)
    packed, usual = portions_of(count, rows * top, bound, skew, True), portions_of(count, rows * top, bound, skew, False)
    places = jnp.arange(count)

    def named(tallies, rotation):
        used = int((tallies > 0).sum())
        fixed = max(1, used // 4)
        shifted = fixed + (places - fixed + rotation * (used - fixed)) % max(1, count - fixed)
        return jnp.zeros((count,), jnp.int32).at[sequence[jnp.where(places < fixed, places, shifted)]].set(jnp.asarray(tallies, jnp.int32))

    tallies = jnp.where(number % 4 == 0, named(packed, number // 4), named(usual, number - number // 4 - 1))
    mixed = jax.random.permutation(jax.random.fold_in(own, 3), count)
    source_of, sink = mixed[0:count // 2 * 2:2], mixed[1:count // 2 * 2:2]
    slack = jnp.minimum(tallies[source_of] - 1, bound - tallies[sink]) // 2
    slack = jnp.where((source_of == sequence[0]) | (sink == sequence[0]) | (tallies[sink] == 0), 0, jnp.maximum(slack, 0))
    shifted = jax.random.randint(jax.random.fold_in(own, 4), (count // 2,), 0, 1 << 20) % (slack + 1)
    tallies = tallies.at[source_of].add(-shifted).at[sink].add(shifted)
    members = jnp.searchsorted(jnp.cumsum(tallies), jnp.arange(rows * top), side="right").astype(jnp.int32)
    grid = members.reshape(top, rows).T
    grid = grid[jax.random.permutation(jax.random.fold_in(own, 1), rows)]
    rotation = jax.random.randint(jax.random.fold_in(own, 2), (rows, 1), 0, top)
    return jnp.take_along_axis(grid, (jnp.arange(top)[None, :] + rotation) % top, axis=1)


def portions_of(amount, total, limit, lean, full):
    loads = [(1 << 20) // math.isqrt(grade ** lean) + 1 for grade in range(1, amount + 1)]
    largest = limit if full else min(limit, max(-(-total // amount), total * loads[0] // sum(loads)))
    least = 1 if total - largest >= amount - 1 else 0
    given, surplus = [largest] + [least] * (amount - 1), total - largest - least * (amount - 1)
    while surplus > 0:
        movable = [i for i in range(1, amount) if given[i] < largest] or [i for i in range(1, amount) if given[i] < limit]
        pool, budget = sum([loads[i] for i in movable]), surplus
        for i in movable:
            extra = min(limit - given[i], max(1, budget * loads[i] // pool), surplus)
            given[i] = given[i] + extra
            surplus = surplus - extra
    return np.array(given)


def bell_draw(stream_key, dims, spread, bound, cuts=(), kind=jnp.bfloat16):
    array = spread * jax.random.normal(stream_key, dims, jnp.float32)
    if cuts:
        array = array * steps_of(stream_key, dims, cuts, -0.22, 0.18)
    return jnp.clip(array, -bound, bound).astype(kind)


def setup_inputs(seed: int = 0, part: int = 0) -> dict:
    splits = jax.random.split(jax.random.key(seed), 11)
    part_keys = jax.random.split(jax.random.fold_in(splits[10], part), 11)
    tokens = bell_draw(part_keys[0], (TOKENS, D), 1.0, 6.0, ((0, 16),))
    expert_ids_keys = jax.random.split(jax.random.fold_in(part_keys[1], 1), TOKENS // TOK_DEV)
    expert_ids_turns = jax.random.permutation(jax.random.fold_in(part_keys[1], 3), TOKENS // TOK_DEV)
    expert_ids = jax.vmap(lambda own, number: assign_block(jax.random.fold_in(part_keys[1], 2), own, number, TOK_DEV, ROUTED, TOP, CAP, 2))(expert_ids_keys, expert_ids_turns).reshape((TOKENS, TOP))
    gate_codes = set_ends(jax.random.randint(part_keys[2], (TOKENS, TOP), 1, 32768), jax.random.fold_in(part_keys[2], 1), 1, 32767).astype(jnp.int32)
    cotangent = bell_draw(part_keys[3], (TOKENS, D), 1.0, 6.0, ((0, 16),))
    gate_weight = bell_draw(splits[4], (EXPERTS, D, FF), D ** -0.5, 0.09375, ((0, 4), (1, 4)))
    up_weight = bell_draw(splits[5], (EXPERTS, D, FF), D ** -0.5, 0.09375, ((0, 4), (1, 4)))
    down_weight = bell_draw(splits[6], (EXPERTS, FF, D), FF ** -0.5, 0.1875, ((0, 4), (2, 4)))
    first_moment = bell_draw(part_keys[7], (EXPERTS, FF, D), (0.2 * LIVE ** 0.5), 6.0, ((0, 4), (2, 4)))
    second_moment = jnp.clip(jnp.exp(math.log(6.375) - 2.3038113 * jax.random.uniform(part_keys[8], (EXPERTS, FF, D), jnp.float32) ** steps_of(part_keys[8], (EXPERTS, FF, D), ((0, 4), (2, 4)), -0.2, 0.2)), 0.63671875, 6.375).astype(jnp.bfloat16)
    selected = draw_selected(jax.random.fold_in(jax.random.fold_in(splits[10], part), 71), part)
    return {"tokens": tokens, "expert_ids": expert_ids, "gate_codes": gate_codes, "cotangent": cotangent, "gate_weight": gate_weight, "up_weight": up_weight, "down_weight": down_weight, "first_moment": first_moment, "second_moment": second_moment, "selected": selected}


BETA_ONE = 0.9
BETA_TWO = 0.95
ADAM_EPS = 1e-08

def reference(tokens, expert_ids, gate_codes, cotangent, gate_weight, up_weight, down_weight, first_moment, second_moment, selected):
    blocks = TOKENS // TOK_DEV
    row_total = blocks * CAP
    code_values = gate_codes.astype(jnp.float32)
    gate_rounded = (2.5 * code_values / lax.optimization_barrier(jnp.sum(code_values, axis=1, keepdims=True))).astype(jnp.bfloat16)
    gate_values = lax.optimization_barrier(gate_rounded).astype(jnp.float32)
    cot_float = cotangent.astype(jnp.float32)
    block_of = jnp.arange(TOKENS, dtype=jnp.int32) // TOK_DEV

    def expert_pass(totals, expert):
        mixed_acc, grad_acc = totals
        matched = expert_ids == expert
        counts = lax.optimization_barrier(jnp.sum(matched.astype(jnp.int32), axis=1))
        gate_each = lax.optimization_barrier(jnp.sum(jnp.where(matched, gate_values, 0.0), axis=1))
        per_block = counts.reshape(blocks, TOK_DEV)
        before = (jnp.cumsum(per_block, axis=1) - per_block).reshape(TOKENS)
        slot_index = jnp.where(counts > 0, block_of * CAP + before, row_total).astype(jnp.int32)
        rows_x = jnp.zeros((row_total, D), jnp.bfloat16).at[slot_index].set(tokens, mode='drop')
        grad_rows = (gate_each[:, None] * cot_float).astype(jnp.bfloat16)
        rows_dy = jnp.zeros((row_total, D), jnp.bfloat16).at[slot_index].set(grad_rows, mode='drop')
        w_gate = gate_weight[expert]
        w_up = up_weight[expert]
        w_down = down_weight[expert]
        gate_pre = jnp.dot(rows_x, w_gate, preferred_element_type=jnp.float32)
        up_pre = jnp.dot(rows_x, w_up, preferred_element_type=jnp.float32)
        sigmoid_gate = jax.nn.sigmoid(gate_pre)
        hidden = (jax.nn.silu(gate_pre) * up_pre).astype(jnp.bfloat16)
        out_rows = jnp.dot(hidden, w_down, preferred_element_type=jnp.float32).astype(jnp.bfloat16)
        hidden_grad = jnp.dot(rows_dy, w_down.T, preferred_element_type=jnp.float32)
        gate_grad = (hidden_grad * up_pre * sigmoid_gate * (1.0 + gate_pre * (1.0 - sigmoid_gate))).astype(jnp.bfloat16)
        up_grad = (hidden_grad * gate_pre * sigmoid_gate).astype(jnp.bfloat16)
        row_grad = (jnp.dot(gate_grad, w_gate.T, preferred_element_type=jnp.float32) + jnp.dot(up_grad, w_up.T, preferred_element_type=jnp.float32)).astype(jnp.bfloat16)
        clamped = jnp.minimum(slot_index, row_total - 1)
        mixed_acc = mixed_acc + gate_each[:, None] * out_rows[clamped].astype(jnp.float32)
        grad_acc = grad_acc + jnp.where(counts[:, None] > 0, row_grad[clamped].astype(jnp.float32), 0.0)
        down_grad = jnp.dot(hidden.T, rows_dy, preferred_element_type=jnp.float32)
        chosen = jnp.any(selected == expert)
        old_one = first_moment[expert].astype(jnp.float32)
        old_two = second_moment[expert].astype(jnp.float32)
        moment_one = BETA_ONE * old_one + (1.0 - BETA_ONE) * down_grad
        moment_two = BETA_TWO * old_two + (1.0 - BETA_TWO) * down_grad * down_grad
        direction = moment_one / (jnp.sqrt(moment_two) + ADAM_EPS)
        adam_step = jnp.where(chosen, direction, 0.0).astype(jnp.bfloat16)
        out_one = jnp.where(chosen, moment_one, old_one).astype(jnp.bfloat16)
        out_two = jnp.where(chosen, moment_two, old_two).astype(jnp.bfloat16)
        return ((mixed_acc, grad_acc), (adam_step, out_one, out_two))
    start_totals = (jnp.zeros((TOKENS, D), jnp.float32), jnp.zeros((TOKENS, D), jnp.float32))
    totals, stacked = lax.scan(expert_pass, start_totals, jnp.arange(EXPERTS, dtype=jnp.int32))
    mixed = totals[0].astype(jnp.bfloat16)
    input_grad = totals[1].astype(jnp.bfloat16)
    return (mixed, input_grad, stacked[0], stacked[1], stacked[2])
```

```python
import functools

import jax
import jax.numpy as jnp
from jax import lax
from jax.experimental import pallas as pl
from jax.experimental.pallas import tpu as pltpu
from jax.sharding import PartitionSpec as P

CAP = 6
CHUNKS = 4
GROUP = 8
LINES = 2 * CHUNKS * CAP
HALF = CHUNKS * CAP

BETA_ONE = 0.9
BETA_TWO = 0.95
ADAM_EPS = 1e-08

F32 = jnp.float32
BF16 = jnp.bfloat16
VMEM = pl.BlockSpec(memory_space=pltpu.VMEM)
SMEM = pl.BlockSpec(memory_space=pltpu.SMEM)
MIB = 1 << 20


def iota(shape, dim):
    return lax.broadcasted_iota(jnp.int32, shape, dim)


def dot(a, b, contract=((1,), (0,))):
    return lax.dot_general(a, b, (contract, ((), ())), preferred_element_type=F32)


def shuffle(backward):
    size = GROUP * LINES
    a, b = iota((size, size), 0), iota((size, size), 1)
    if backward:
        a, b = b, a
    per = GROUP * CAP
    chunk, rest = a // (2 * per), a % (2 * per)
    half, rest = rest // per, rest % per
    source, slot = rest // CAP, rest % CAP
    return (b == source * LINES + half * HALF + chunk * CAP + slot).astype(F32).astype(BF16)


def dispatch_kernel(experts, dp, ids_ref, codes_ref, tok_ref, cot_ref, sent_ref, ones_ref, gates_ref):
    rows = tok_ref.shape[0]
    width = tok_ref.shape[1] // dp // CHUNKS
    codes = codes_ref[...].astype(F32)
    gates = (2.5 * codes / jnp.sum(codes, axis=0, keepdims=True)).astype(BF16).astype(F32)
    ids = ids_ref[...]
    matched = [ids == e for e in range(experts)]
    counts = jnp.concatenate(
        [jnp.sum(m.astype(F32), axis=0, keepdims=True) for m in matched], axis=0
    )
    gate_each = [jnp.sum(jnp.where(m, gates, 0.0), axis=0, keepdims=True) for m in matched]
    earlier = (iota((rows, rows), 0) < iota((rows, rows), 1)).astype(F32).astype(BF16)
    before = dot(counts.astype(BF16), earlier)
    slot8 = iota((8, rows), 0).astype(F32)
    line = iota((HALF, rows), 0)
    slot_of, chunk_of = (line % CAP).astype(F32), line // CAP
    x_rows, dy_rows = [], []
    for e in range(experts):
        taken = counts[e : e + 1] > 0
        at8 = taken & (before[e : e + 1] == slot8)
        ones_ref[e * 8 : e * 8 + 8, :] = at8.astype(F32)
        gates_ref[e * 8 : e * 8 + 8, :] = jnp.where(at8, gate_each[e], 0.0)
        at = taken & (before[e : e + 1] == slot_of)
        x_rows.append(
            jnp.concatenate([(at & (chunk_of == c)).astype(F32) for c in range(CHUNKS)], axis=1)
        )
        dy_rows.append(
            jnp.concatenate(
                [jnp.where(at & (chunk_of == c), gate_each[e], 0.0) for c in range(CHUNKS)], axis=1
            )
        )
    x_rows = jnp.concatenate(x_rows, axis=0).astype(BF16)
    dy_rows = jnp.concatenate(dy_rows, axis=0).astype(BF16)
    for j in range(dp):
        base = j * width * CHUNKS
        pieces = [slice(base + c * width, base + (c + 1) * width) for c in range(CHUNKS)]
        out_x = dot(x_rows, jnp.concatenate([tok_ref[:, p] for p in pieces], axis=0))
        out_dy = dot(dy_rows, jnp.concatenate([cot_ref[:, p] for p in pieces], axis=0))
        for e in range(experts):
            part = slice(e * HALF, (e + 1) * HALF)
            sent_ref[e * dp + j] = jnp.concatenate([out_x[part], out_dy[part]], axis=0).astype(BF16)


def partial_kernel(dp, arrived_ref, gate_w, up_w, down_w, own_ref, *refs):
    sent = refs[: dp - 1]
    rows_dy, rows_x, total = refs[dp - 1 :]
    me = lax.axis_index("dp")
    sources, _, width = arrived_ref.shape
    block = total.shape[2] // dp
    order = shuffle(False)
    per = GROUP * CAP
    for g in range(sources // GROUP):
        lines = jnp.concatenate(
            [arrived_ref[g * GROUP + i] for i in range(GROUP)], axis=0
        )
        sorted_lines = dot(order, lines).astype(BF16)
        for c in range(CHUNKS):
            for half, target in ((0, rows_x), (1, rows_dy)):
                start = (c * 2 + half) * per
                target[g * per : (g + 1) * per, c * width : (c + 1) * width] = sorted_lines[
                    start : start + per
                ]
    total[0] = dot(rows_x[...], gate_w[0])
    total[1] = dot(rows_x[...], up_w[0])
    total[2] = dot(rows_dy[...], down_w[0], ((1,), (1,)))
    for k in range(dp):
        at = pl.multiple_of(jnp.bitwise_xor(me, k) * block, block)
        part = total[:, :, pl.ds(at, block)]
        if k == 0:
            own_ref[...] = part
        else:
            sent[k - 1][...] = part.astype(BF16)


def hidden_kernel(own_ref, *refs):
    arrived, share_ref = refs[:-1], refs[-1]
    gate, up, grad = [
        sum([r[i].astype(F32) for r in arrived], own_ref[i]) for i in range(3)
    ]
    sig = jax.nn.sigmoid(gate)
    share_ref[0] = (gate * sig * up).astype(BF16)
    share_ref[1] = (grad * up * sig * (1.0 + gate * (1.0 - sig))).astype(BF16)
    share_ref[2] = (grad * gate * sig).astype(BF16)


def result_kernel(dp, share_ref, *refs):
    arrived = (share_ref,) + refs[: dp - 1]
    gate_w, up_w, down_w, sent_ref, hidden_ref, full = refs[dp - 1 :]
    me = lax.axis_index("dp")
    sources, _, width = sent_ref.shape
    block = share_ref.shape[2]
    for k in range(dp):
        at = pl.multiple_of(jnp.bitwise_xor(me, k) * block, block)
        hidden_ref[:, pl.ds(at, block)] = arrived[k][0]
        full[0, :, pl.ds(at, block)] = arrived[k][1]
        full[1, :, pl.ds(at, block)] = arrived[k][2]
    out = dot(hidden_ref[...], down_w[0]).astype(BF16)
    grad = (
        dot(full[0], gate_w[0], ((1,), (1,))) + dot(full[1], up_w[0], ((1,), (1,)))
    ).astype(BF16)
    order = shuffle(True)
    per = GROUP * CAP
    for g in range(sources // GROUP):
        lines = jnp.concatenate(
            [
                value[g * per : (g + 1) * per, c * width : (c + 1) * width]
                for c in range(CHUNKS)
                for value in (out, grad)
            ],
            axis=0,
        )
        sorted_lines = dot(order, lines).astype(BF16)
        for i in range(GROUP):
            sent_ref[g * GROUP + i] = sorted_lines[i * LINES : (i + 1) * LINES]


def adam_kernel(selected_ref, hidden_ref, dy_ref, first_ref, second_ref, step_ref, one_ref, two_ref):
    me = lax.axis_index("expert")
    chosen = selected_ref[0] == me
    for i in range(1, selected_ref.shape[0]):
        chosen = chosen | (selected_ref[i] == me)

    @pl.when(chosen)
    def _():
        grad = dot(hidden_ref[...], dy_ref[...], ((0,), (0,)))
        one = BETA_ONE * first_ref[0].astype(F32) + (1.0 - BETA_ONE) * grad
        two = BETA_TWO * second_ref[0].astype(F32) + (1.0 - BETA_TWO) * grad * grad
        step_ref[0] = (one / (jnp.sqrt(two) + ADAM_EPS)).astype(BF16)
        one_ref[0] = one.astype(BF16)
        two_ref[0] = two.astype(BF16)

    @pl.when(jnp.logical_not(chosen))
    def _():
        step_ref[...] = jnp.zeros_like(step_ref)
        one_ref[...] = first_ref[...]
        two_ref[...] = second_ref[...]


def combine_kernel(experts, dp, ones_ref, gates_ref, back_ref, mixed_ref, grad_ref):
    width = back_ref.shape[2]
    small = (experts * 8, experts * LINES)
    source, target = iota(small, 0), iota(small, 1)
    same = (source // 8 == target // LINES) & (source % 8 < CAP)
    within = target % LINES
    ones, gates = ones_ref[...].astype(BF16), gates_ref[...].astype(BF16)
    spreads = []
    for half, value in ((0, gates), (1, ones)):
        for c in range(CHUNKS):
            spot = same & (within == half * HALF + c * CAP + source % 8)
            spreads.append(dot(value, spot.astype(F32).astype(BF16), ((0,), (0,))).astype(BF16))
    for j in range(dp):
        lines = jnp.concatenate([back_ref[e * dp + j] for e in range(experts)], axis=0)
        for half, ref in ((0, mixed_ref), (1, grad_ref)):
            for c in range(CHUNKS):
                at = (j * CHUNKS + c) * width
                ref[:, at : at + width] = dot(spreads[half * CHUNKS + c], lines).astype(BF16)


def call(kernel, outs, operands, in_specs=None, scratch=(), limit=40, flops=0, traffic=0):
    return pl.pallas_call(
        kernel,
        out_shape=outs,
        in_specs=in_specs or [VMEM] * len(operands),
        out_specs=jax.tree.map(lambda _: VMEM, outs),
        scratch_shapes=scratch,
        compiler_params=pltpu.CompilerParams(vmem_limit_bytes=limit * MIB),
        cost_estimate=pl.CostEstimate(flops=flops, bytes_accessed=traffic, transcendentals=0),
    )(*operands)


def local(
    tokens,
    expert_ids,
    gate_codes,
    cotangent,
    gate_weight,
    up_weight,
    down_weight,
    first_moment,
    second_moment,
    selected,
):
    experts = lax.axis_size("expert")
    dp = lax.axis_size("dp")
    tok_rows, model = tokens.shape
    slice_width = model // dp
    width = slice_width // CHUNKS
    hidden_units = gate_weight.shape[2]
    block = hidden_units // dp
    sources = experts * dp
    slots = sources * CAP
    shape = jax.ShapeDtypeStruct
    cube = slots * slice_width * hidden_units

    sent, ones, gates = call(
        functools.partial(dispatch_kernel, experts, dp),
        (
            shape((sources, LINES, width), BF16),
            shape((experts * 8, tok_rows), F32),
            shape((experts * 8, tok_rows), F32),
        ),
        (expert_ids.T, gate_codes.T, tokens, cotangent),
        traffic=6 * MIB,
    )
    arrived = lax.all_to_all(sent, ("expert", "dp"), split_axis=0, concat_axis=0, tiled=True)

    def swap(value, k):
        return lax.ppermute(value, "dp", [(i, i ^ k) for i in range(dp)])

    own, *rest = call(
        functools.partial(partial_kernel, dp),
        (shape((3, slots, block), F32),)
        + (shape((3, slots, block), BF16),) * (dp - 1)
        + (shape((slots, slice_width), BF16),),
        (arrived, gate_weight, up_weight, down_weight),
        scratch=[
            pltpu.VMEM((slots, slice_width), BF16),
            pltpu.VMEM((3, slots, hidden_units), F32),
        ],
        flops=6 * cube,
        traffic=8 * MIB,
    )
    rows_dy = rest[-1]
    sums = [swap(rest[k - 1], k) for k in range(1, dp)]
    share = call(
        hidden_kernel, shape((3, slots, block), BF16), (own, *sums), traffic=2 * MIB
    )
    shares = [swap(share, k) for k in range(1, dp)]
    results, hidden = call(
        functools.partial(result_kernel, dp),
        (shape((sources, LINES, width), BF16), shape((slots, hidden_units), BF16)),
        (share, *shares, gate_weight, up_weight, down_weight),
        scratch=[pltpu.VMEM((2, slots, hidden_units), BF16)],
        flops=6 * cube,
        traffic=8 * MIB,
    )
    back = lax.all_to_all(results, ("expert", "dp"), split_axis=0, concat_axis=0, tiled=True)

    strip = hidden_units // 8
    moments = pl.BlockSpec((1, strip, slice_width), lambda i: (0, i, 0))
    adam = pl.pallas_call(
        adam_kernel,
        grid=(hidden_units // strip,),
        in_specs=[
            SMEM,
            pl.BlockSpec((slots, strip), lambda i: (0, i)),
            pl.BlockSpec((slots, slice_width), lambda i: (0, 0)),
            moments,
            moments,
        ],
        out_specs=(moments, moments, moments),
        out_shape=(shape(first_moment.shape, BF16),) * 3,
        compiler_params=pltpu.CompilerParams(vmem_limit_bytes=40 * MIB),
        cost_estimate=pl.CostEstimate(
            flops=2 * cube, bytes_accessed=10 * MIB, transcendentals=hidden_units * slice_width
        ),
    )(selected, hidden, rows_dy, first_moment, second_moment)

    mixed, input_grad = call(
        functools.partial(combine_kernel, experts, dp),
        (shape((tok_rows, model), BF16), shape((tok_rows, model), BF16)),
        (ones, gates, back),
        traffic=4 * MIB,
    )
    return (mixed, input_grad, *adam)


def solution(mesh):
    placed = (
        P(("groups", "expert", "dp"), None),
        P(("groups", "expert", "dp"), None),
        P(("groups", "expert", "dp"), None),
        P(("groups", "expert", "dp"), None),
        P("expert", "dp", None),
        P("expert", "dp", None),
        P("expert", None, "dp"),
        P(("groups", "expert"), None, "dp"),
        P(("groups", "expert"), None, "dp"),
        P("groups"),
    )
    return jax.shard_map(
        local,
        mesh=mesh,
        in_specs=placed,
        out_specs=(
            P(("groups", "expert", "dp"), None),
            P(("groups", "expert", "dp"), None),
            P(("groups", "expert"), None, "dp"),
            P(("groups", "expert"), None, "dp"),
            P(("groups", "expert"), None, "dp"),
        ),
        check_vma=False,
    )
```

```python
import functools

import jax
import jax.numpy as jnp
from jax import lax
from jax.experimental import pallas as pl
from jax.experimental.pallas import tpu as pltpu
from jax.sharding import PartitionSpec as P

CAP = 6
CHUNKS = 4
GROUP = 8
LINES = 2 * CHUNKS * CAP
HALF = CHUNKS * CAP

BETA_ONE = 0.9
BETA_TWO = 0.95
ADAM_EPS = 1e-08

F32 = jnp.float32
BF16 = jnp.bfloat16
VMEM = pl.BlockSpec(memory_space=pltpu.VMEM)
SMEM = pl.BlockSpec(memory_space=pltpu.SMEM)
MIB = 1 << 20
MOST = 60


def iota(shape, dim):
    return lax.broadcasted_iota(jnp.int32, shape, dim)


def dot(a, b, contract=((1,), (0,))):
    return lax.dot_general(a, b, (contract, ((), ())), preferred_element_type=F32)


def onehot(vector, size, dim):
    return (iota(size, dim) == vector).astype(F32).astype(BF16)


def gather_rows(arrived_ref, targets):
    sources, _, width = arrived_ref.shape
    per, size = GROUP * CAP, GROUP * LINES
    line = iota((1, size), 1)
    source, rest = line // LINES, line % LINES
    order = onehot(rest // CAP * per + source * CAP + rest % CAP, (size, size), 0)
    for g in range(sources // GROUP):
        lines = jnp.concatenate([arrived_ref[g * GROUP + i] for i in range(GROUP)], axis=0)
        sorted_lines = dot(order, lines).astype(BF16)
        for half, target in enumerate(targets):
            for c in range(CHUNKS):
                start = (half * CHUNKS + c) * per
                target[g * per : (g + 1) * per, c * width : (c + 1) * width] = sorted_lines[
                    start : start + per
                ]


def scatter_rows(values, sent_ref):
    sources, _, width = sent_ref.shape
    per, size = GROUP * CAP, GROUP * LINES
    row = iota((1, size), 1)
    part, rest = row // per, row % per
    order = onehot(rest // CAP * LINES + part * CAP + rest % CAP, (size, size), 0)
    for g in range(sources // GROUP):
        lines = jnp.concatenate(
            [
                value[g * per : (g + 1) * per, c * width : (c + 1) * width]
                for value in values
                for c in range(CHUNKS)
            ],
            axis=0,
        )
        sorted_lines = dot(order, lines).astype(BF16)
        for i in range(GROUP):
            sent_ref[g * GROUP + i] = sorted_lines[i * LINES : (i + 1) * LINES]


def dispatch_kernel(
    experts, dp, ids_hbm, codes_hbm, tok_hbm, cot_hbm, sent_ref, ones_ref, gates_ref,
    ids_ref, codes_ref, tok_ref, cot_ref, sems,
):
    copies = [
        pltpu.make_async_copy(a, b, sems.at[i])
        for i, (a, b) in enumerate(
            (
                (ids_hbm, ids_ref),
                (codes_hbm, codes_ref),
                (tok_hbm, tok_ref),
                (cot_hbm, cot_ref),
            )
        )
    ]
    for c in copies:
        c.start()
    rows = tok_ref.shape[0]
    width = tok_ref.shape[1] // dp // CHUNKS
    earlier = (iota((rows, rows), 0) < iota((rows, rows), 1)).astype(F32).astype(BF16)
    copies[0].wait()
    copies[1].wait()
    codes = codes_ref[...].astype(F32)
    gates = (2.5 * codes / jnp.sum(codes, axis=0, keepdims=True)).astype(BF16).astype(F32)
    ids = ids_ref[...]
    matched = [ids == e for e in range(experts)]
    counts = jnp.concatenate(
        [jnp.sum(m.astype(F32), axis=0, keepdims=True) for m in matched], axis=0
    )
    gate_each = [jnp.sum(jnp.where(m, gates, 0.0), axis=0, keepdims=True) for m in matched]
    before = dot(counts.astype(BF16), earlier)
    slot8 = iota((8, rows), 0).astype(F32)
    line = iota((HALF, rows), 0)
    slot_of, chunk_of = (line % CAP).astype(F32), line // CAP
    x_rows, dy_rows = [], []
    for e in range(experts):
        taken = counts[e : e + 1] > 0
        at8 = taken & (before[e : e + 1] == slot8)
        ones_ref[e * 8 : e * 8 + 8, :] = at8.astype(F32)
        gates_ref[e * 8 : e * 8 + 8, :] = jnp.where(at8, gate_each[e], 0.0)
        at = taken & (before[e : e + 1] == slot_of)
        x_rows.append(
            jnp.concatenate([(at & (chunk_of == c)).astype(F32) for c in range(CHUNKS)], axis=1)
        )
        dy_rows.append(
            jnp.concatenate(
                [jnp.where(at & (chunk_of == c), gate_each[e], 0.0) for c in range(CHUNKS)], axis=1
            )
        )
    x_rows = jnp.concatenate(x_rows, axis=0).astype(BF16)
    dy_rows = jnp.concatenate(dy_rows, axis=0).astype(BF16)
    for copy, source_ref, weights, half in (
        (copies[2], tok_ref, x_rows, 0),
        (copies[3], cot_ref, dy_rows, HALF),
    ):
        copy.wait()
        for j in range(dp):
            base = j * width * CHUNKS
            lines = jnp.concatenate(
                [
                    source_ref[:, base + c * width : base + (c + 1) * width]
                    for c in range(CHUNKS)
                ],
                axis=0,
            )
            out = dot(weights, lines)
            for e in range(experts):
                sent_ref[e * dp + j, half : half + HALF] = out[
                    e * HALF : (e + 1) * HALF
                ].astype(BF16)


def backward_kernel(arrived_ref, down_w, rows_x, rows_dy, total):
    gather_rows(arrived_ref, (rows_x, rows_dy))
    total[...] = dot(rows_dy[...], down_w[0], ((1,), (1,)))


def forward_kernel(dp, rows_x, grad_ref, gate_w, up_w, own_ref, *refs):
    sent, (total,) = refs[: dp - 1], refs[dp - 1 :]
    total[0] = dot(rows_x[...], gate_w[0])
    total[1] = dot(rows_x[...], up_w[0])
    me = lax.axis_index("dp")
    block = total.shape[2] // dp
    for k in range(dp):
        at = pl.ds(pl.multiple_of(jnp.bitwise_xor(me, k) * block, block), block)
        target = own_ref if k == 0 else sent[k - 1]
        target[:2] = total[:, :, at].astype(target.dtype)
        target[2] = grad_ref[:, at].astype(target.dtype)


def summed(refs, i):
    return sum([r[i].astype(F32) for r in refs[1:]], refs[0][i])


def share_kernel(*refs):
    sums, share_ref = refs[:-1], refs[-1]
    gate, up, grad = [summed(sums, i) for i in range(3)]
    sig = jax.nn.sigmoid(gate)
    share_ref[0] = (gate * sig * up).astype(BF16)
    share_ref[1] = (grad * up * sig * (1.0 + gate * (1.0 - sig))).astype(BF16)
    share_ref[2] = (grad * gate * sig).astype(BF16)


def result_kernel(dp, *refs):
    arrived = refs[:dp]
    gate_w, up_w, down_w, sent_ref, hidden_ref, full = refs[dp:]
    me = lax.axis_index("dp")
    block = arrived[0].shape[2]
    for k in range(dp):
        at = pl.multiple_of(jnp.bitwise_xor(me, k) * block, block)
        hidden_ref[:, pl.ds(at, block)] = arrived[k][0]
        full[:, :, pl.ds(at, block)] = arrived[k][1:]
    out = dot(hidden_ref[...], down_w[0])
    grad = dot(full[0], gate_w[0], ((1,), (1,))) + dot(full[1], up_w[0], ((1,), (1,)))
    scatter_rows((out.astype(BF16), grad.astype(BF16)), sent_ref)


def adam_kernel(selected_ref, hidden_ref, dy_ref, first_ref, second_ref, step_ref, one_ref, two_ref):
    me = lax.axis_index("expert")
    chosen = selected_ref[0] == me
    for i in range(1, selected_ref.shape[0]):
        chosen = chosen | (selected_ref[i] == me)

    @pl.when(chosen)
    def _():
        grad = dot(hidden_ref[...], dy_ref[...], ((0,), (0,)))
        one = BETA_ONE * first_ref[0].astype(F32) + (1.0 - BETA_ONE) * grad
        two = BETA_TWO * second_ref[0].astype(F32) + (1.0 - BETA_TWO) * grad * grad
        step_ref[0] = (one / (jnp.sqrt(two) + ADAM_EPS)).astype(BF16)
        one_ref[0] = one.astype(BF16)
        two_ref[0] = two.astype(BF16)

    @pl.when(jnp.logical_not(chosen))
    def _():
        step_ref[...] = jnp.zeros_like(step_ref)
        one_ref[...] = first_ref[...]
        two_ref[...] = second_ref[...]


def combine_kernel(
    experts, dp, ones_ref, gates_ref, back_ref, mixed_hbm, grad_hbm, mixed_ref, grad_ref, sems
):
    _, lines_each, width = back_ref.shape
    small = (experts * 8, experts * lines_each)
    source, target = iota(small, 0), iota(small, 1)
    same = (source // 8 == target // lines_each) & (source % 8 < CAP)
    within = target % lines_each
    spreads = []
    for half, ref in ((0, gates_ref), (1, ones_ref)):
        weights = ref[...].astype(BF16)
        for c in range(CHUNKS):
            spot = same & (within == half * HALF + c * CAP + source % 8)
            spreads.append(dot(weights, spot.astype(F32).astype(BF16), ((0,), (0,))).astype(BF16))
    copies = []
    for j in range(dp):
        lines = jnp.concatenate([back_ref[e * dp + j] for e in range(experts)], axis=0)
        for half, ref, hbm in ((0, mixed_ref, mixed_hbm), (1, grad_ref, grad_hbm)):
            for c in range(CHUNKS):
                at = (j * CHUNKS + c) * width
                ref[:, at : at + width] = dot(spreads[half * CHUNKS + c], lines).astype(BF16)
            span = pl.ds(j * CHUNKS * width, CHUNKS * width)
            copies.append(
                pltpu.make_async_copy(
                    ref.at[:, span], hbm.at[:, span], sems.at[half, j]
                )
            )
            copies[-1].start()
    for c in copies:
        c.wait()


def call(kernel, outs, operands, in_specs=None, out_specs=None, scratch=(), limit=24, flops=0, traffic=0):
    return pl.pallas_call(
        kernel,
        out_shape=outs,
        in_specs=in_specs or [VMEM] * len(operands),
        out_specs=out_specs or jax.tree.map(lambda _: VMEM, outs),
        scratch_shapes=scratch,
        compiler_params=pltpu.CompilerParams(vmem_limit_bytes=limit * MIB),
        cost_estimate=pl.CostEstimate(flops=flops, bytes_accessed=traffic, transcendentals=0),
    )(*operands)


def local(
    tokens,
    expert_ids,
    gate_codes,
    cotangent,
    gate_weight,
    up_weight,
    down_weight,
    first_moment,
    second_moment,
    selected,
):
    experts = lax.axis_size("expert")
    dp = lax.axis_size("dp")
    tok_rows, model = tokens.shape
    slice_width = model // dp
    width = slice_width // CHUNKS
    hidden_units = gate_weight.shape[2]
    block = hidden_units // dp
    sources = experts * dp
    slots = sources * CAP
    shape = jax.ShapeDtypeStruct
    cube = slots * slice_width * hidden_units
    own_specs = [pl.BlockSpec(memory_space=pltpu.HBM)] * 4

    sent, ones, gates = call(
        functools.partial(dispatch_kernel, experts, dp),
        (
            shape((sources, LINES, width), BF16),
            shape((experts * 8, tok_rows), F32),
            shape((experts * 8, tok_rows), F32),
        ),
        (expert_ids.T, gate_codes.T, tokens, cotangent),
        in_specs=own_specs,
        limit=MOST,
        scratch=[
            pltpu.VMEM(expert_ids.shape[::-1], jnp.int32),
            pltpu.VMEM(gate_codes.shape[::-1], jnp.int32),
            pltpu.VMEM(tokens.shape, BF16),
            pltpu.VMEM(cotangent.shape, BF16),
            pltpu.SemaphoreType.DMA((4,)),
        ],
        traffic=6 * MIB,
    )
    arrived = lax.all_to_all(sent, ("expert", "dp"), split_axis=0, concat_axis=0, tiled=True)
    def swap(value, k):
        return lax.ppermute(value, "dp", [(i, i ^ k) for i in range(dp)])

    def swaps(values):
        return [swap(values[k - 1], k) for k in range(1, dp)]

    weights = (gate_weight, up_weight, down_weight)

    rows_x, rows_dy, grad_parts = call(
        backward_kernel,
        (
            shape((slots, slice_width), BF16),
            shape((slots, slice_width), BF16),
            shape((slots, hidden_units), F32),
        ),
        (arrived, down_weight),
        flops=2 * cube,
        traffic=3 * MIB,
    )
    own, *parts = call(
        functools.partial(forward_kernel, dp),
        (shape((3, slots, block), F32),) + (shape((3, slots, block), BF16),) * (dp - 1),
        (rows_x, grad_parts, gate_weight, up_weight),
        scratch=[pltpu.VMEM((2, slots, hidden_units), F32)],
        flops=4 * cube,
        traffic=6 * MIB,
    )
    sums = [own, *swaps(parts)]
    share = call(
        share_kernel,
        shape((3, slots, block), BF16),
        sums,
        traffic=MIB,
    )
    shares = swaps([share] * (dp - 1))
    results, hidden = call(
        functools.partial(result_kernel, dp),
        (shape((sources, LINES, width), BF16), shape((slots, hidden_units), BF16)),
        (share, *shares, *weights),
        scratch=[pltpu.VMEM((2, slots, hidden_units), BF16)],
        flops=6 * cube,
        traffic=8 * MIB,
    )
    back = lax.all_to_all(results, ("expert", "dp"), split_axis=0, concat_axis=0, tiled=True)

    strip = hidden_units // 8
    moments = pl.BlockSpec((1, strip, slice_width), lambda i: (0, i, 0))
    adam = pl.pallas_call(
        adam_kernel,
        grid=(hidden_units // strip,),
        in_specs=[
            SMEM,
            pl.BlockSpec((slots, strip), lambda i: (0, i)),
            pl.BlockSpec((slots, slice_width), lambda i: (0, 0)),
            moments,
            moments,
        ],
        out_specs=(moments, moments, moments),
        out_shape=(shape(first_moment.shape, BF16),) * 3,
        compiler_params=pltpu.CompilerParams(vmem_limit_bytes=32 * MIB),
        cost_estimate=pl.CostEstimate(
            flops=2 * cube, bytes_accessed=10 * MIB, transcendentals=hidden_units * slice_width
        ),
    )(selected, hidden, rows_dy, first_moment, second_moment)

    mixed, input_grad = call(
        functools.partial(combine_kernel, experts, dp),
        (shape((tok_rows, model), BF16), shape((tok_rows, model), BF16)),
        (ones, gates, back),
        out_specs=(own_specs[0],) * 2,
        scratch=[
            pltpu.VMEM((tok_rows, model), BF16),
            pltpu.VMEM((tok_rows, model), BF16),
            pltpu.SemaphoreType.DMA((2, dp)),
        ],
        traffic=4 * MIB,
    )
    return (mixed, input_grad, *adam)


def solution(mesh):
    placed = (
        P(("groups", "expert", "dp"), None),
        P(("groups", "expert", "dp"), None),
        P(("groups", "expert", "dp"), None),
        P(("groups", "expert", "dp"), None),
        P("expert", "dp", None),
        P("expert", "dp", None),
        P("expert", None, "dp"),
        P(("groups", "expert"), None, "dp"),
        P(("groups", "expert"), None, "dp"),
        P("groups"),
    )
    return jax.shard_map(
        local,
        mesh=mesh,
        in_specs=placed,
        out_specs=(
            P(("groups", "expert", "dp"), None),
            P(("groups", "expert", "dp"), None),
            P(("groups", "expert"), None, "dp"),
            P(("groups", "expert"), None, "dp"),
            P(("groups", "expert"), None, "dp"),
        ),
        check_vma=False,
    )
```

```python
import functools

import jax
import jax.numpy as jnp
from jax import lax
from jax.experimental import pallas as pl
from jax.experimental.pallas import tpu as pltpu
from jax.sharding import PartitionSpec as P

CAP = 6
CHUNKS = 4
GROUP = 8
LINES = 2 * CHUNKS * CAP
HALF = CHUNKS * CAP

BETA_ONE = 0.9
BETA_TWO = 0.95
ADAM_EPS = 1e-08

F32 = jnp.float32
BF16 = jnp.bfloat16
VMEM = pl.BlockSpec(memory_space=pltpu.VMEM)
SMEM = pl.BlockSpec(memory_space=pltpu.SMEM)
MIB = 1 << 20
MOST = 58


def iota(shape, dim):
    return lax.broadcasted_iota(jnp.int32, shape, dim)


def dot(a, b, contract=((1,), (0,))):
    return lax.dot_general(a, b, (contract, ((), ())), preferred_element_type=F32)


def onehot(vector, size, dim):
    return (iota(size, dim) == vector).astype(F32).astype(BF16)


def gather_rows(arrived_ref, targets):
    sources, _, width = arrived_ref.shape
    per, size = GROUP * CAP, GROUP * LINES
    line = iota((1, size), 1)
    source, rest = line // LINES, line % LINES
    order = onehot(rest // CAP * per + source * CAP + rest % CAP, (size, size), 0)
    for g in range(sources // GROUP):
        lines = jnp.concatenate([arrived_ref[g * GROUP + i] for i in range(GROUP)], axis=0)
        sorted_lines = dot(order, lines).astype(BF16)
        for half, target in enumerate(targets):
            for c in range(CHUNKS):
                start = (half * CHUNKS + c) * per
                target[g * per : (g + 1) * per, c * width : (c + 1) * width] = sorted_lines[
                    start : start + per
                ]


def scatter_rows(values, sent_ref):
    sources, _, width = sent_ref.shape
    per, size = GROUP * CAP, GROUP * LINES
    row = iota((1, size), 1)
    part, rest = row // per, row % per
    order = onehot(rest // CAP * LINES + part * CAP + rest % CAP, (size, size), 0)
    for g in range(sources // GROUP):
        lines = jnp.concatenate(
            [
                value[g * per : (g + 1) * per, c * width : (c + 1) * width]
                for value in values
                for c in range(CHUNKS)
            ],
            axis=0,
        )
        sorted_lines = dot(order, lines).astype(BF16)
        for i in range(GROUP):
            sent_ref[g * GROUP + i] = sorted_lines[i * LINES : (i + 1) * LINES]


def dispatch_kernel(
    experts, dp, ids_hbm, codes_hbm, tok_hbm, cot_hbm, sent_ref, ones_ref, gates_ref,
    ids_ref, codes_ref, tok_ref, cot_ref, sems,
):
    copies = [
        pltpu.make_async_copy(a, b, sems.at[i])
        for i, (a, b) in enumerate(
            (
                (ids_hbm, ids_ref),
                (codes_hbm, codes_ref),
                (tok_hbm, tok_ref),
                (cot_hbm, cot_ref),
            )
        )
    ]
    for c in copies:
        c.start()
    rows = tok_ref.shape[0]
    width = tok_ref.shape[1] // dp // CHUNKS
    earlier = (iota((rows, rows), 0) < iota((rows, rows), 1)).astype(F32).astype(BF16)
    copies[0].wait()
    copies[1].wait()
    codes = codes_ref[...].astype(F32)
    gates = (2.5 * codes / jnp.sum(codes, axis=0, keepdims=True)).astype(BF16).astype(F32)
    ids = ids_ref[...]
    matched = [ids == e for e in range(experts)]
    counts = jnp.concatenate(
        [jnp.sum(m.astype(F32), axis=0, keepdims=True) for m in matched], axis=0
    )
    gate_each = [jnp.sum(jnp.where(m, gates, 0.0), axis=0, keepdims=True) for m in matched]
    before = dot(counts.astype(BF16), earlier)
    slot8 = iota((8, rows), 0).astype(F32)
    line = iota((HALF, rows), 0)
    slot_of, chunk_of = (line % CAP).astype(F32), line // CAP
    x_rows, dy_rows = [], []
    for e in range(experts):
        taken = counts[e : e + 1] > 0
        at8 = taken & (before[e : e + 1] == slot8)
        ones_ref[e * 8 : e * 8 + 8, :] = at8.astype(F32)
        gates_ref[e * 8 : e * 8 + 8, :] = jnp.where(at8, gate_each[e], 0.0)
        at = taken & (before[e : e + 1] == slot_of)
        x_rows.append(
            jnp.concatenate([(at & (chunk_of == c)).astype(F32) for c in range(CHUNKS)], axis=1)
        )
        dy_rows.append(
            jnp.concatenate(
                [jnp.where(at & (chunk_of == c), gate_each[e], 0.0) for c in range(CHUNKS)], axis=1
            )
        )
    x_rows = jnp.concatenate(x_rows, axis=0).astype(BF16)
    dy_rows = jnp.concatenate(dy_rows, axis=0).astype(BF16)
    for copy, source_ref, weights, half in (
        (copies[2], tok_ref, x_rows, 0),
        (copies[3], cot_ref, dy_rows, HALF),
    ):
        copy.wait()
        for j in range(dp):
            base = j * width * CHUNKS
            lines = jnp.concatenate(
                [
                    source_ref[:, base + c * width : base + (c + 1) * width]
                    for c in range(CHUNKS)
                ],
                axis=0,
            )
            out = dot(weights, lines)
            for e in range(experts):
                sent_ref[e * dp + j, half : half + HALF] = out[
                    e * HALF : (e + 1) * HALF
                ].astype(BF16)


def gather_kernel(arrived_ref, rows_x, rows_dy):
    gather_rows(arrived_ref, (rows_x, rows_dy))


def backward_kernel(rows_dy, down_w, total):
    total[...] = dot(rows_dy[...], down_w[0], ((1,), (1,)))


def forward_kernel(dp, rows_x, grad_ref, gate_w, up_w, own_ref, *refs):
    sent, (total,) = refs[: dp - 1], refs[dp - 1 :]
    total[0] = dot(rows_x[...], gate_w[0])
    total[1] = dot(rows_x[...], up_w[0])
    me = lax.axis_index("dp")
    block = total.shape[2] // dp
    for k in range(dp):
        at = pl.ds(pl.multiple_of(jnp.bitwise_xor(me, k) * block, block), block)
        target = own_ref if k == 0 else sent[k - 1]
        target[:2] = total[:, :, at].astype(target.dtype)
        target[2] = grad_ref[:, at].astype(target.dtype)


def summed(refs, i):
    return sum([r[i].astype(F32) for r in refs[1:]], refs[0][i])


def share_kernel(*refs):
    sums, share_ref = refs[:-1], refs[-1]
    gate, up, grad = [summed(sums, i) for i in range(3)]
    sig = jax.nn.sigmoid(gate)
    share_ref[0] = (gate * sig * up).astype(BF16)
    share_ref[1] = (grad * up * sig * (1.0 + gate * (1.0 - sig))).astype(BF16)
    share_ref[2] = (grad * gate * sig).astype(BF16)


def turn_kernel(*refs):
    count = len(refs) // 2
    for source, target in zip(refs[:count], refs[count:]):
        target[...] = source[0].T


def result_kernel(dp, *refs):
    arrived = refs[:dp]
    gate_w, up_w, down_w, sent_ref, hidden_ref, full = refs[dp:]
    me = lax.axis_index("dp")
    block = arrived[0].shape[2]
    for k in range(dp):
        at = pl.multiple_of(jnp.bitwise_xor(me, k) * block, block)
        hidden_ref[:, pl.ds(at, block)] = arrived[k][0]
        full[:, :, pl.ds(at, block)] = arrived[k][1:]
    out = dot(hidden_ref[...], down_w[0])
    grad = dot(full[0], gate_w[...]) + dot(full[1], up_w[...])
    scatter_rows((out.astype(BF16), grad.astype(BF16)), sent_ref)


def adam_kernel(selected_ref, hidden_ref, dy_ref, first_ref, second_ref, step_ref, one_ref, two_ref):
    me = lax.axis_index("expert")
    chosen = selected_ref[0] == me
    for i in range(1, selected_ref.shape[0]):
        chosen = chosen | (selected_ref[i] == me)

    @pl.when(chosen)
    def _():
        grad = dot(hidden_ref[...], dy_ref[...], ((0,), (0,)))
        one = BETA_ONE * first_ref[0].astype(F32) + (1.0 - BETA_ONE) * grad
        two = BETA_TWO * second_ref[0].astype(F32) + (1.0 - BETA_TWO) * grad * grad
        step_ref[0] = (one / (jnp.sqrt(two) + ADAM_EPS)).astype(BF16)
        one_ref[0] = one.astype(BF16)
        two_ref[0] = two.astype(BF16)

    @pl.when(jnp.logical_not(chosen))
    def _():
        step_ref[...] = jnp.zeros_like(step_ref)
        one_ref[...] = first_ref[...]
        two_ref[...] = second_ref[...]


def combine_kernel(
    experts, dp, ones_ref, gates_ref, back_ref, mixed_hbm, grad_hbm, mixed_ref, grad_ref, sems
):
    width = back_ref.shape[2]
    small = (experts * 8, experts * LINES)
    source, target = iota(small, 0), iota(small, 1)
    same = (source // 8 == target // LINES) & (source % 8 < CAP)
    within = target % LINES - source % 8
    spreads = []
    for half, ref in ((0, gates_ref), (1, ones_ref)):
        weights = ref[...].astype(BF16)
        for c in range(CHUNKS):
            spot = same & (within == half * HALF + c * CAP)
            spreads.append(dot(weights, spot.astype(F32).astype(BF16), ((0,), (0,))).astype(BF16))
    copies = []
    for j in range(dp):
        lines = jnp.concatenate([back_ref[e * dp + j] for e in range(experts)], axis=0)
        for half, ref, hbm in ((0, mixed_ref, mixed_hbm), (1, grad_ref, grad_hbm)):
            for c in range(CHUNKS):
                at = (j * CHUNKS + c) * width
                ref[:, at : at + width] = dot(spreads[half * CHUNKS + c], lines).astype(BF16)
            span = pl.ds(j * CHUNKS * width, CHUNKS * width)
            copies.append(pltpu.make_async_copy(ref.at[:, span], hbm.at[:, span], sems.at[half, j]))
            copies[-1].start()
    for c in copies:
        c.wait()


def call(kernel, outs, operands, in_specs=None, out_specs=None, scratch=(), limit=24, flops=0, traffic=0):
    return pl.pallas_call(
        kernel,
        out_shape=outs,
        in_specs=in_specs or [VMEM] * len(operands),
        out_specs=out_specs or jax.tree.map(lambda _: VMEM, outs),
        scratch_shapes=scratch,
        compiler_params=pltpu.CompilerParams(vmem_limit_bytes=int(limit * MIB)),
        cost_estimate=pl.CostEstimate(flops=flops, bytes_accessed=traffic, transcendentals=0),
    )(*operands)


def local(
    tokens,
    expert_ids,
    gate_codes,
    cotangent,
    gate_weight,
    up_weight,
    down_weight,
    first_moment,
    second_moment,
    selected,
):
    experts = lax.axis_size("expert")
    dp = lax.axis_size("dp")
    tok_rows, model = tokens.shape
    slice_width = model // dp
    width = slice_width // CHUNKS
    hidden_units = gate_weight.shape[2]
    block = hidden_units // dp
    sources = experts * dp
    slots = sources * CAP
    shape = jax.ShapeDtypeStruct
    cube = slots * slice_width * hidden_units
    own_specs = [pl.BlockSpec(memory_space=pltpu.HBM)] * 4

    sent, ones, gates = call(
        functools.partial(dispatch_kernel, experts, dp),
        (
            shape((sources, LINES, width), BF16),
            shape((experts * 8, tok_rows), F32),
            shape((experts * 8, tok_rows), F32),
        ),
        (expert_ids.T, gate_codes.T, tokens, cotangent),
        in_specs=own_specs,
        limit=MOST,
        scratch=[
            pltpu.VMEM(expert_ids.shape[::-1], jnp.int32),
            pltpu.VMEM(gate_codes.shape[::-1], jnp.int32),
            pltpu.VMEM(tokens.shape, BF16),
            pltpu.VMEM(cotangent.shape, BF16),
            pltpu.SemaphoreType.DMA((4,)),
        ],
        traffic=6 * MIB,
    )
    arrived = lax.all_to_all(sent, ("expert", "dp"), split_axis=0, concat_axis=0, tiled=True)
    def swap(value, k):
        return lax.ppermute(value, "dp", [(i, i ^ k) for i in range(dp)])

    def swaps(values):
        return [swap(values[k - 1], k) for k in range(1, dp)]

    weights = (gate_weight, up_weight, down_weight)

    rows_x, rows_dy = call(
        gather_kernel,
        (shape((slots, slice_width), BF16), shape((slots, slice_width), BF16)),
        (arrived,),
        flops=5 * 10**8,
        traffic=MIB // 2,
    )
    grad_parts = call(
        backward_kernel,
        shape((slots, hidden_units), F32),
        (rows_dy, down_weight),
        flops=5 * 10**8,
        traffic=MIB // 8,
    )
    own, *parts = call(
        functools.partial(forward_kernel, dp),
        (shape((3, slots, block), F32),) + (shape((3, slots, block), BF16),) * (dp - 1),
        (rows_x, grad_parts, gate_weight, up_weight),
        scratch=[pltpu.VMEM((2, slots, hidden_units), F32)],
        flops=4 * cube,
        traffic=6 * MIB,
    )
    sums = [own, *swaps(parts)]
    turned = call(
        turn_kernel,
        (shape((hidden_units, slice_width), BF16),) * 2,
        (gate_weight, up_weight),
        traffic=4 * MIB,
    )
    own, *turned = lax.optimization_barrier((own, *turned))
    sums[0] = own
    share = call(
        share_kernel,
        shape((3, slots, block), BF16),
        sums,
        traffic=MIB,
    )
    shares = swaps([share] * (dp - 1))
    results, hidden = call(
        functools.partial(result_kernel, dp),
        (shape((sources, LINES, width), BF16), shape((slots, hidden_units), BF16)),
        (share, *shares, *turned, down_weight),
        scratch=[pltpu.VMEM((2, slots, hidden_units), BF16)],
        flops=6 * cube,
        traffic=8 * MIB,
    )
    back = lax.all_to_all(results, ("expert", "dp"), split_axis=0, concat_axis=0, tiled=True)

    strip = hidden_units // 8
    moments = pl.BlockSpec((1, strip, slice_width), lambda i: (0, i, 0))
    adam = pl.pallas_call(
        adam_kernel,
        grid=(hidden_units // strip,),
        in_specs=[
            SMEM,
            pl.BlockSpec((slots, strip), lambda i: (0, i)),
            pl.BlockSpec((slots, slice_width), lambda i: (0, 0)),
            moments,
            moments,
        ],
        out_specs=(moments, moments, moments),
        out_shape=(shape(first_moment.shape, BF16),) * 3,
        compiler_params=pltpu.CompilerParams(vmem_limit_bytes=32 * MIB),
        cost_estimate=pl.CostEstimate(
            flops=2 * cube, bytes_accessed=10 * MIB, transcendentals=hidden_units * slice_width
        ),
    )(selected, hidden, rows_dy, first_moment, second_moment)

    mixed, input_grad = call(
        functools.partial(combine_kernel, experts, dp),
        (shape((tok_rows, model), BF16), shape((tok_rows, model), BF16)),
        (ones, gates, back),
        out_specs=(own_specs[0],) * 2,
        scratch=[
            pltpu.VMEM((tok_rows, model), BF16),
            pltpu.VMEM((tok_rows, model), BF16),
            pltpu.SemaphoreType.DMA((2, dp)),
        ],
        traffic=4 * MIB,
    )
    return (mixed, input_grad, *adam)


def solution(mesh):
    placed = (
        P(("groups", "expert", "dp"), None),
        P(("groups", "expert", "dp"), None),
        P(("groups", "expert", "dp"), None),
        P(("groups", "expert", "dp"), None),
        P("expert", "dp", None),
        P("expert", "dp", None),
        P("expert", None, "dp"),
        P(("groups", "expert"), None, "dp"),
        P(("groups", "expert"), None, "dp"),
        P("groups"),
    )
    return jax.shard_map(
        local,
        mesh=mesh,
        in_specs=placed,
        out_specs=(
            P(("groups", "expert", "dp"), None),
            P(("groups", "expert", "dp"), None),
            P(("groups", "expert"), None, "dp"),
            P(("groups", "expert"), None, "dp"),
            P(("groups", "expert"), None, "dp"),
        ),
        check_vma=False,
    )
```

```python
import functools

import jax
import jax.numpy as jnp
from jax import lax
from jax.experimental import pallas as pl
from jax.experimental.pallas import tpu as pltpu
from jax.sharding import PartitionSpec as P

CAP = 6
CHUNKS = 4
GROUP = 8
LINES = 2 * CHUNKS * CAP
HALF = CHUNKS * CAP

BETA_ONE = 0.9
BETA_TWO = 0.95
ADAM_EPS = 1e-08

F32 = jnp.float32
BF16 = jnp.bfloat16
VMEM = pl.BlockSpec(memory_space=pltpu.VMEM)
SMEM = pl.BlockSpec(memory_space=pltpu.SMEM)
MIB = 1 << 20
MOST = 58
GF = 5 * 10**8
GU = 3 * 10**8


def iota(shape, dim):
    return lax.broadcasted_iota(jnp.int32, shape, dim)


def dot(a, b, contract=((1,), (0,))):
    return lax.dot_general(a, b, (contract, ((), ())), preferred_element_type=F32)


def onehot(vector, size, dim):
    return (iota(size, dim) == vector).astype(F32).astype(BF16)


def gather_rows(arrived_ref, targets):
    sources, _, width = arrived_ref.shape
    per, size = GROUP * CAP, GROUP * LINES
    line = iota((1, size), 1)
    source, rest = line // LINES, line % LINES
    order = onehot(rest // CAP * per + source * CAP + rest % CAP, (size, size), 0)
    for g in range(sources // GROUP):
        lines = jnp.concatenate([arrived_ref[g * GROUP + i] for i in range(GROUP)], axis=0)
        sorted_lines = dot(order, lines).astype(BF16)
        for half, target in enumerate(targets):
            for c in range(CHUNKS):
                start = (half * CHUNKS + c) * per
                target[g * per : (g + 1) * per, c * width : (c + 1) * width] = sorted_lines[
                    start : start + per
                ]


def scatter_rows(values, sent_ref):
    sources, _, width = sent_ref.shape
    per, size = GROUP * CAP, GROUP * LINES
    row = iota((1, size), 1)
    part, rest = row // per, row % per
    order = onehot(rest // CAP * LINES + part * CAP + rest % CAP, (size, size), 0)
    for g in range(sources // GROUP):
        lines = jnp.concatenate(
            [
                value[g * per : (g + 1) * per, c * width : (c + 1) * width]
                for value in values
                for c in range(CHUNKS)
            ],
            axis=0,
        )
        sorted_lines = dot(order, lines).astype(BF16)
        for i in range(GROUP):
            sent_ref[g * GROUP + i] = sorted_lines[i * LINES : (i + 1) * LINES]


def dispatch_kernel(
    experts, dp, ids_hbm, codes_hbm, tok_hbm, cot_hbm, sent_ref, ones_ref, gates_ref,
    ids_ref, codes_ref, tok_ref, cot_ref, sems,
):
    copies = [
        pltpu.make_async_copy(a, b, sems.at[i])
        for i, (a, b) in enumerate(
            (
                (ids_hbm, ids_ref),
                (codes_hbm, codes_ref),
                (tok_hbm, tok_ref),
                (cot_hbm, cot_ref),
            )
        )
    ]
    for c in copies:
        c.start()
    rows = tok_ref.shape[0]
    width = tok_ref.shape[1] // dp // CHUNKS
    earlier = (iota((rows, rows), 0) < iota((rows, rows), 1)).astype(F32).astype(BF16)
    copies[0].wait()
    copies[1].wait()
    codes = codes_ref[...].astype(F32)
    gates = (2.5 * codes / jnp.sum(codes, axis=0, keepdims=True)).astype(BF16).astype(F32)
    ids = ids_ref[...]
    matched = [ids == e for e in range(experts)]
    counts = jnp.concatenate(
        [jnp.sum(m.astype(F32), axis=0, keepdims=True) for m in matched], axis=0
    )
    gate_each = [jnp.sum(jnp.where(m, gates, 0.0), axis=0, keepdims=True) for m in matched]
    before = dot(counts.astype(BF16), earlier)
    slot8 = iota((8, rows), 0).astype(F32)
    line = iota((HALF, rows), 0)
    slot_of, chunk_of = (line % CAP).astype(F32), line // CAP
    x_rows, dy_rows = [], []
    for e in range(experts):
        taken = counts[e : e + 1] > 0
        at8 = taken & (before[e : e + 1] == slot8)
        ones_ref[e * 8 : e * 8 + 8, :] = at8.astype(F32)
        gates_ref[e * 8 : e * 8 + 8, :] = jnp.where(at8, gate_each[e], 0.0)
        at = taken & (before[e : e + 1] == slot_of)
        x_rows.append(
            jnp.concatenate([(at & (chunk_of == c)).astype(F32) for c in range(CHUNKS)], axis=1)
        )
        dy_rows.append(
            jnp.concatenate(
                [jnp.where(at & (chunk_of == c), gate_each[e], 0.0) for c in range(CHUNKS)], axis=1
            )
        )
    x_rows = jnp.concatenate(x_rows, axis=0).astype(BF16)
    dy_rows = jnp.concatenate(dy_rows, axis=0).astype(BF16)
    for copy, source_ref, weights, half in (
        (copies[2], tok_ref, x_rows, 0),
        (copies[3], cot_ref, dy_rows, HALF),
    ):
        copy.wait()
        for j in range(dp):
            base = j * width * CHUNKS
            lines = jnp.concatenate(
                [
                    source_ref[:, base + c * width : base + (c + 1) * width]
                    for c in range(CHUNKS)
                ],
                axis=0,
            )
            out = dot(weights, lines)
            for e in range(experts):
                sent_ref[e * dp + j, half : half + HALF] = out[
                    e * HALF : (e + 1) * HALF
                ].astype(BF16)


def gather_kernel(arrived_ref, rows_x, rows_dy):
    gather_rows(arrived_ref, (rows_x, rows_dy))


def forward_kernel(rows_x, gate_w, up_w, total):
    total[0] = dot(rows_x[...], gate_w[0])
    total[1] = dot(rows_x[...], up_w[0])


def backward_kernel(dp, rows_dy, pre_ref, down_w, own_ref, *refs):
    sent, (total,) = refs[: dp - 1], refs[dp - 1 :]
    total[...] = dot(rows_dy[...], down_w[0], ((1,), (1,)))
    me = lax.axis_index("dp")
    block = total.shape[1] // dp
    for k in range(dp):
        at = pl.ds(pl.multiple_of(jnp.bitwise_xor(me, k) * block, block), block)
        target = own_ref if k == 0 else sent[k - 1]
        target[:2] = pre_ref[:, :, at].astype(target.dtype)
        target[2] = total[:, at].astype(target.dtype)


def summed(refs, i):
    return sum([r[i].astype(F32) for r in refs[1:]], refs[0][i])


def share_kernel(*refs):
    sums, share_ref = refs[:-1], refs[-1]
    gate, up, grad = [summed(sums, i) for i in range(3)]
    sig = jax.nn.sigmoid(gate)
    share_ref[0] = (gate * sig * up).astype(BF16)
    share_ref[1] = (grad * up * sig * (1.0 + gate * (1.0 - sig))).astype(BF16)
    share_ref[2] = (grad * gate * sig).astype(BF16)


def turn_kernel(*refs):
    count = len(refs) // 2
    for source, target in zip(refs[:count], refs[count:]):
        target[...] = source[0].T


def result_kernel(dp, *refs):
    arrived = refs[:dp]
    gate_w, up_w, down_w, sent_ref, hidden_ref, full = refs[dp:]
    me = lax.axis_index("dp")
    block = arrived[0].shape[2]
    for k in range(dp):
        at = pl.multiple_of(jnp.bitwise_xor(me, k) * block, block)
        hidden_ref[:, pl.ds(at, block)] = arrived[k][0]
        full[:, :, pl.ds(at, block)] = arrived[k][1:]
    out = dot(hidden_ref[...], down_w[0])
    grad = dot(full[0], gate_w[...]) + dot(full[1], up_w[...])
    scatter_rows((out.astype(BF16), grad.astype(BF16)), sent_ref)


def adam_kernel(selected_ref, hidden_ref, dy_ref, first_ref, second_ref, step_ref, one_ref, two_ref):
    me = lax.axis_index("expert")
    chosen = selected_ref[0] == me
    for i in range(1, selected_ref.shape[0]):
        chosen = chosen | (selected_ref[i] == me)

    @pl.when(chosen)
    def _():
        grad = dot(hidden_ref[...], dy_ref[...], ((0,), (0,)))
        one = BETA_ONE * first_ref[0].astype(F32) + (1.0 - BETA_ONE) * grad
        two = BETA_TWO * second_ref[0].astype(F32) + (1.0 - BETA_TWO) * grad * grad
        step_ref[0] = (one / (jnp.sqrt(two) + ADAM_EPS)).astype(BF16)
        one_ref[0] = one.astype(BF16)
        two_ref[0] = two.astype(BF16)

    @pl.when(jnp.logical_not(chosen))
    def _():
        step_ref[...] = jnp.zeros_like(step_ref)
        one_ref[...] = first_ref[...]
        two_ref[...] = second_ref[...]


def combine_kernel(
    experts, dp, ones_ref, gates_ref, back_ref, mixed_hbm, grad_hbm, mixed_ref, grad_ref, sems
):
    width = back_ref.shape[2]
    small = (experts * 8, experts * LINES)
    source, target = iota(small, 0), iota(small, 1)
    same = (source // 8 == target // LINES) & (source % 8 < CAP)
    within = target % LINES - source % 8
    spreads = []
    for half, ref in ((0, gates_ref), (1, ones_ref)):
        weights = ref[...].astype(BF16)
        for c in range(CHUNKS):
            spot = same & (within == half * HALF + c * CAP)
            spreads.append(dot(weights, spot.astype(F32).astype(BF16), ((0,), (0,))).astype(BF16))
    copies = []
    for j in range(dp):
        lines = jnp.concatenate([back_ref[e * dp + j] for e in range(experts)], axis=0)
        for half, ref, hbm in ((0, mixed_ref, mixed_hbm), (1, grad_ref, grad_hbm)):
            for c in range(CHUNKS):
                at = (j * CHUNKS + c) * width
                ref[:, at : at + width] = dot(spreads[half * CHUNKS + c], lines).astype(BF16)
            span = pl.ds(j * CHUNKS * width, CHUNKS * width)
            copies.append(pltpu.make_async_copy(ref.at[:, span], hbm.at[:, span], sems.at[half, j]))
            copies[-1].start()
    for c in copies:
        c.wait()


def call(kernel, outs, operands, in_specs=None, out_specs=None, scratch=(), limit=24, flops=0, traffic=0):
    return pl.pallas_call(
        kernel,
        out_shape=outs,
        in_specs=in_specs or [VMEM] * len(operands),
        out_specs=out_specs or jax.tree.map(lambda _: VMEM, outs),
        scratch_shapes=scratch,
        compiler_params=pltpu.CompilerParams(vmem_limit_bytes=int(limit * MIB)),
        cost_estimate=pl.CostEstimate(flops=flops, bytes_accessed=traffic, transcendentals=0),
    )(*operands)


def local(
    tokens,
    expert_ids,
    gate_codes,
    cotangent,
    gate_weight,
    up_weight,
    down_weight,
    first_moment,
    second_moment,
    selected,
):
    experts = lax.axis_size("expert")
    dp = lax.axis_size("dp")
    tok_rows, model = tokens.shape
    slice_width = model // dp
    width = slice_width // CHUNKS
    hidden_units = gate_weight.shape[2]
    block = hidden_units // dp
    sources = experts * dp
    slots = sources * CAP
    shape = jax.ShapeDtypeStruct
    cube = slots * slice_width * hidden_units
    own_specs = [pl.BlockSpec(memory_space=pltpu.HBM)] * 4

    sent, ones, gates = call(
        functools.partial(dispatch_kernel, experts, dp),
        (
            shape((sources, LINES, width), BF16),
            shape((experts * 8, tok_rows), F32),
            shape((experts * 8, tok_rows), F32),
        ),
        (expert_ids.T, gate_codes.T, tokens, cotangent),
        in_specs=own_specs,
        limit=MOST,
        scratch=[
            pltpu.VMEM(expert_ids.shape[::-1], jnp.int32),
            pltpu.VMEM(gate_codes.shape[::-1], jnp.int32),
            pltpu.VMEM(tokens.shape, BF16),
            pltpu.VMEM(cotangent.shape, BF16),
            pltpu.SemaphoreType.DMA((4,)),
        ],
        traffic=6 * MIB,
    )
    arrived = lax.all_to_all(sent, ("expert", "dp"), split_axis=0, concat_axis=0, tiled=True)
    def swap(value, k):
        return lax.ppermute(value, "dp", [(i, i ^ k) for i in range(dp)])

    def swaps(values):
        return [swap(values[k - 1], k) for k in range(1, dp)]

    weights = (gate_weight, up_weight, down_weight)

    rows_x, rows_dy = call(
        gather_kernel,
        (shape((slots, slice_width), BF16), shape((slots, slice_width), BF16)),
        (arrived,),
        flops=GF,
        traffic=MIB // 2,
    )
    pre_parts = call(
        forward_kernel,
        shape((2, slots, hidden_units), F32),
        (rows_x, gate_weight, up_weight),
        flops=GU,
        traffic=MIB // 8,
    )
    own, *parts = call(
        functools.partial(backward_kernel, dp),
        (shape((3, slots, block), F32),) + (shape((3, slots, block), BF16),) * (dp - 1),
        (rows_dy, pre_parts, down_weight),
        scratch=[pltpu.VMEM((slots, hidden_units), F32)],
        flops=5 * 10**8,
        traffic=MIB // 8,
    )
    sums = [own, *swaps(parts)]
    turned = call(
        turn_kernel,
        (shape((hidden_units, slice_width), BF16),) * 2,
        (gate_weight, up_weight),
        traffic=4 * MIB,
    )
    own, *turned = lax.optimization_barrier((own, *turned))
    sums[0] = own
    share = call(
        share_kernel,
        shape((3, slots, block), BF16),
        sums,
        traffic=MIB,
    )
    shares = swaps([share] * (dp - 1))
    results, hidden = call(
        functools.partial(result_kernel, dp),
        (shape((sources, LINES, width), BF16), shape((slots, hidden_units), BF16)),
        (share, *shares, *turned, down_weight),
        scratch=[pltpu.VMEM((2, slots, hidden_units), BF16)],
        flops=6 * cube,
        traffic=8 * MIB,
    )
    back = lax.all_to_all(results, ("expert", "dp"), split_axis=0, concat_axis=0, tiled=True)

    strip = hidden_units // 8
    moments = pl.BlockSpec((1, strip, slice_width), lambda i: (0, i, 0))
    adam = pl.pallas_call(
        adam_kernel,
        grid=(hidden_units // strip,),
        in_specs=[
            SMEM,
            pl.BlockSpec((slots, strip), lambda i: (0, i)),
            pl.BlockSpec((slots, slice_width), lambda i: (0, 0)),
            moments,
            moments,
        ],
        out_specs=(moments, moments, moments),
        out_shape=(shape(first_moment.shape, BF16),) * 3,
        compiler_params=pltpu.CompilerParams(vmem_limit_bytes=32 * MIB),
        cost_estimate=pl.CostEstimate(
            flops=2 * cube, bytes_accessed=10 * MIB, transcendentals=hidden_units * slice_width
        ),
    )(selected, hidden, rows_dy, first_moment, second_moment)

    mixed, input_grad = call(
        functools.partial(combine_kernel, experts, dp),
        (shape((tok_rows, model), BF16), shape((tok_rows, model), BF16)),
        (ones, gates, back),
        out_specs=(own_specs[0],) * 2,
        scratch=[
            pltpu.VMEM((tok_rows, model), BF16),
            pltpu.VMEM((tok_rows, model), BF16),
            pltpu.SemaphoreType.DMA((2, dp)),
        ],
        traffic=4 * MIB,
    )
    return (mixed, input_grad, *adam)


def solution(mesh):
    placed = (
        P(("groups", "expert", "dp"), None),
        P(("groups", "expert", "dp"), None),
        P(("groups", "expert", "dp"), None),
        P(("groups", "expert", "dp"), None),
        P("expert", "dp", None),
        P("expert", "dp", None),
        P("expert", None, "dp"),
        P(("groups", "expert"), None, "dp"),
        P(("groups", "expert"), None, "dp"),
        P("groups"),
    )
    return jax.shard_map(
        local,
        mesh=mesh,
        in_specs=placed,
        out_specs=(
            P(("groups", "expert", "dp"), None),
            P(("groups", "expert", "dp"), None),
            P(("groups", "expert"), None, "dp"),
            P(("groups", "expert"), None, "dp"),
            P(("groups", "expert"), None, "dp"),
        ),
        check_vma=False,
    )
```

```python
import functools

import jax
import jax.numpy as jnp
from jax import lax
from jax.experimental import pallas as pl
from jax.experimental.pallas import tpu as pltpu
from jax.sharding import PartitionSpec as P

CAP = 6
CHUNKS = 4
GROUP = 8
LINES = 2 * CHUNKS * CAP
HALF = CHUNKS * CAP

BETA_ONE = 0.9
BETA_TWO = 0.95
ADAM_EPS = 1e-08

F32 = jnp.float32
BF16 = jnp.bfloat16
VMEM = pl.BlockSpec(memory_space=pltpu.VMEM)
SMEM = pl.BlockSpec(memory_space=pltpu.SMEM)
MIB = 1 << 20
RS = (3, 2, 1)
AG = (2, 1, 3)
MOST = 58
GF = 5 * 10**8
GU = 3 * 10**8


def turns(dp, order):
    return order if dp == len(order) + 1 else tuple(range(1, dp))


def iota(shape, dim):
    return lax.broadcasted_iota(jnp.int32, shape, dim)


def dot(a, b, contract=((1,), (0,))):
    return lax.dot_general(a, b, (contract, ((), ())), preferred_element_type=F32)


def onehot(vector, size, dim):
    return (iota(size, dim) == vector).astype(F32).astype(BF16)


def gather_rows(arrived_ref, targets):
    sources, _, width = arrived_ref.shape
    per, size = GROUP * CAP, GROUP * LINES
    line = iota((1, size), 1)
    source, rest = line // LINES, line % LINES
    order = onehot(rest // CAP * per + source * CAP + rest % CAP, (size, size), 0)
    for g in range(sources // GROUP):
        lines = jnp.concatenate([arrived_ref[g * GROUP + i] for i in range(GROUP)], axis=0)
        sorted_lines = dot(order, lines).astype(BF16)
        for half, target in enumerate(targets):
            for c in range(CHUNKS):
                start = (half * CHUNKS + c) * per
                target[g * per : (g + 1) * per, c * width : (c + 1) * width] = sorted_lines[
                    start : start + per
                ]


def scatter_rows(values, sent_ref):
    sources, _, width = sent_ref.shape
    per, size = GROUP * CAP, GROUP * LINES
    row = iota((1, size), 1)
    part, rest = row // per, row % per
    order = onehot(rest // CAP * LINES + part * CAP + rest % CAP, (size, size), 0)
    for g in range(sources // GROUP):
        lines = jnp.concatenate(
            [
                value[g * per : (g + 1) * per, c * width : (c + 1) * width]
                for value in values
                for c in range(CHUNKS)
            ],
            axis=0,
        )
        sorted_lines = dot(order, lines).astype(BF16)
        for i in range(GROUP):
            sent_ref[g * GROUP + i] = sorted_lines[i * LINES : (i + 1) * LINES]


def dispatch_kernel(
    experts, dp, ids_hbm, codes_hbm, tok_hbm, cot_hbm, sent_ref, ones_ref, gates_ref,
    ids_ref, codes_ref, tok_ref, cot_ref, sems,
):
    copies = [
        pltpu.make_async_copy(a, b, sems.at[i])
        for i, (a, b) in enumerate(
            (
                (ids_hbm, ids_ref),
                (codes_hbm, codes_ref),
                (tok_hbm, tok_ref),
                (cot_hbm, cot_ref),
            )
        )
    ]
    for c in copies:
        c.start()
    rows = tok_ref.shape[0]
    width = tok_ref.shape[1] // dp // CHUNKS
    earlier = (iota((rows, rows), 0) < iota((rows, rows), 1)).astype(F32).astype(BF16)
    copies[0].wait()
    copies[1].wait()
    codes = codes_ref[...].astype(F32)
    gates = (2.5 * codes / jnp.sum(codes, axis=0, keepdims=True)).astype(BF16).astype(F32)
    ids = ids_ref[...]
    matched = [ids == e for e in range(experts)]
    counts = jnp.concatenate(
        [jnp.sum(m.astype(F32), axis=0, keepdims=True) for m in matched], axis=0
    )
    gate_each = [jnp.sum(jnp.where(m, gates, 0.0), axis=0, keepdims=True) for m in matched]
    before = dot(counts.astype(BF16), earlier)
    slot8 = iota((8, rows), 0).astype(F32)
    line = iota((HALF, rows), 0)
    slot_of, chunk_of = (line % CAP).astype(F32), line // CAP
    x_rows, dy_rows = [], []
    for e in range(experts):
        taken = counts[e : e + 1] > 0
        at8 = taken & (before[e : e + 1] == slot8)
        ones_ref[e * 8 : e * 8 + 8, :] = at8.astype(F32)
        gates_ref[e * 8 : e * 8 + 8, :] = jnp.where(at8, gate_each[e], 0.0)
        at = taken & (before[e : e + 1] == slot_of)
        x_rows.append(
            jnp.concatenate([(at & (chunk_of == c)).astype(F32) for c in range(CHUNKS)], axis=1)
        )
        dy_rows.append(
            jnp.concatenate(
                [jnp.where(at & (chunk_of == c), gate_each[e], 0.0) for c in range(CHUNKS)], axis=1
            )
        )
    x_rows = jnp.concatenate(x_rows, axis=0).astype(BF16)
    dy_rows = jnp.concatenate(dy_rows, axis=0).astype(BF16)
    for copy, source_ref, weights, half in (
        (copies[2], tok_ref, x_rows, 0),
        (copies[3], cot_ref, dy_rows, HALF),
    ):
        copy.wait()
        for j in range(dp):
            base = j * width * CHUNKS
            lines = jnp.concatenate(
                [
                    source_ref[:, base + c * width : base + (c + 1) * width]
                    for c in range(CHUNKS)
                ],
                axis=0,
            )
            out = dot(weights, lines)
            for e in range(experts):
                sent_ref[e * dp + j, half : half + HALF] = out[
                    e * HALF : (e + 1) * HALF
                ].astype(BF16)


def gather_kernel(arrived_ref, rows_x, rows_dy):
    gather_rows(arrived_ref, (rows_x, rows_dy))


def forward_kernel(rows_x, gate_w, up_w, total):
    total[0] = dot(rows_x[...], gate_w[0])
    total[1] = dot(rows_x[...], up_w[0])


def backward_kernel(dp, rows_dy, pre_ref, down_w, own_ref, *refs):
    sent, (total,) = refs[: dp - 1], refs[dp - 1 :]
    total[...] = dot(rows_dy[...], down_w[0], ((1,), (1,)))
    me = lax.axis_index("dp")
    block = total.shape[1] // dp
    for k in range(dp):
        at = pl.ds(pl.multiple_of(jnp.bitwise_xor(me, k) * block, block), block)
        target = own_ref if k == 0 else sent[k - 1]
        target[:2] = pre_ref[:, :, at].astype(target.dtype)
        target[2] = total[:, at].astype(target.dtype)


def summed(refs, i):
    return sum([r[i].astype(F32) for r in refs[1:]], refs[0][i])


def share_kernel(*refs):
    sums, share_ref = refs[:-1], refs[-1]
    gate, up, grad = [summed(sums, i) for i in range(3)]
    sig = jax.nn.sigmoid(gate)
    share_ref[0] = (gate * sig * up).astype(BF16)
    share_ref[1] = (grad * up * sig * (1.0 + gate * (1.0 - sig))).astype(BF16)
    share_ref[2] = (grad * gate * sig).astype(BF16)


def turn_kernel(*refs):
    count = len(refs) // 2
    for source, target in zip(refs[:count], refs[count:]):
        target[...] = source[0].T


def result_kernel(dp, *refs):
    arrived = refs[:dp]
    order = (0, *turns(dp, AG))
    gate_w, up_w, down_w, sent_ref, hidden_ref, full = refs[dp:]
    me = lax.axis_index("dp")
    block = arrived[0].shape[2]
    for i, k in enumerate(order):
        at = pl.multiple_of(jnp.bitwise_xor(me, k) * block, block)
        hidden_ref[:, pl.ds(at, block)] = arrived[i][0]
        full[:, :, pl.ds(at, block)] = arrived[i][1:]
    out = dot(hidden_ref[...], down_w[0])
    grad = dot(full[0], gate_w[...]) + dot(full[1], up_w[...])
    scatter_rows((out.astype(BF16), grad.astype(BF16)), sent_ref)


def adam_kernel(selected_ref, hidden_ref, dy_ref, first_ref, second_ref, step_ref, one_ref, two_ref):
    me = lax.axis_index("expert")
    chosen = selected_ref[0] == me
    for i in range(1, selected_ref.shape[0]):
        chosen = chosen | (selected_ref[i] == me)

    @pl.when(chosen)
    def _():
        grad = dot(hidden_ref[...], dy_ref[...], ((0,), (0,)))
        one = BETA_ONE * first_ref[0].astype(F32) + (1.0 - BETA_ONE) * grad
        two = BETA_TWO * second_ref[0].astype(F32) + (1.0 - BETA_TWO) * grad * grad
        step_ref[0] = (one / (jnp.sqrt(two) + ADAM_EPS)).astype(BF16)
        one_ref[0] = one.astype(BF16)
        two_ref[0] = two.astype(BF16)

    @pl.when(jnp.logical_not(chosen))
    def _():
        step_ref[...] = jnp.zeros_like(step_ref)
        one_ref[...] = first_ref[...]
        two_ref[...] = second_ref[...]


def combine_kernel(
    experts, dp, ones_ref, gates_ref, back_ref, mixed_hbm, grad_hbm, mixed_ref, grad_ref, sems
):
    width = back_ref.shape[2]
    small = (experts * 8, experts * LINES)
    source, target = iota(small, 0), iota(small, 1)
    same = (source // 8 == target // LINES) & (source % 8 < CAP)
    within = target % LINES - source % 8
    spreads = []
    for half, ref in ((0, gates_ref), (1, ones_ref)):
        weights = ref[...].astype(BF16)
        for c in range(CHUNKS):
            spot = same & (within == half * HALF + c * CAP)
            spreads.append(dot(weights, spot.astype(F32).astype(BF16), ((0,), (0,))).astype(BF16))
    copies = []
    for j in range(dp):
        lines = jnp.concatenate([back_ref[e * dp + j] for e in range(experts)], axis=0)
        for half, ref, hbm in ((0, mixed_ref, mixed_hbm), (1, grad_ref, grad_hbm)):
            for c in range(CHUNKS):
                at = (j * CHUNKS + c) * width
                ref[:, at : at + width] = dot(spreads[half * CHUNKS + c], lines).astype(BF16)
            span = pl.ds(j * CHUNKS * width, CHUNKS * width)
            copies.append(pltpu.make_async_copy(ref.at[:, span], hbm.at[:, span], sems.at[half, j]))
            copies[-1].start()
    for c in copies:
        c.wait()


def call(kernel, outs, operands, in_specs=None, out_specs=None, scratch=(), limit=24, flops=0, traffic=0):
    return pl.pallas_call(
        kernel,
        out_shape=outs,
        in_specs=in_specs or [VMEM] * len(operands),
        out_specs=out_specs or jax.tree.map(lambda _: VMEM, outs),
        scratch_shapes=scratch,
        compiler_params=pltpu.CompilerParams(vmem_limit_bytes=int(limit * MIB)),
        cost_estimate=pl.CostEstimate(flops=flops, bytes_accessed=traffic, transcendentals=0),
    )(*operands)


def local(
    tokens,
    expert_ids,
    gate_codes,
    cotangent,
    gate_weight,
    up_weight,
    down_weight,
    first_moment,
    second_moment,
    selected,
):
    experts = lax.axis_size("expert")
    dp = lax.axis_size("dp")
    tok_rows, model = tokens.shape
    slice_width = model // dp
    width = slice_width // CHUNKS
    hidden_units = gate_weight.shape[2]
    block = hidden_units // dp
    sources = experts * dp
    slots = sources * CAP
    shape = jax.ShapeDtypeStruct
    cube = slots * slice_width * hidden_units
    own_specs = [pl.BlockSpec(memory_space=pltpu.HBM)] * 4

    sent, ones, gates = call(
        functools.partial(dispatch_kernel, experts, dp),
        (
            shape((sources, LINES, width), BF16),
            shape((experts * 8, tok_rows), F32),
            shape((experts * 8, tok_rows), F32),
        ),
        (expert_ids.T, gate_codes.T, tokens, cotangent),
        in_specs=own_specs,
        limit=MOST,
        scratch=[
            pltpu.VMEM(expert_ids.shape[::-1], jnp.int32),
            pltpu.VMEM(gate_codes.shape[::-1], jnp.int32),
            pltpu.VMEM(tokens.shape, BF16),
            pltpu.VMEM(cotangent.shape, BF16),
            pltpu.SemaphoreType.DMA((4,)),
        ],
        traffic=6 * MIB,
    )
    arrived = lax.all_to_all(sent, ("expert", "dp"), split_axis=0, concat_axis=0, tiled=True)
    def swap(value, k):
        return lax.ppermute(value, "dp", [(i, i ^ k) for i in range(dp)])

    def swaps(values):
        return [swap(values[k - 1], k) for k in range(1, dp)]

    weights = (gate_weight, up_weight, down_weight)

    rows_x, rows_dy = call(
        gather_kernel,
        (shape((slots, slice_width), BF16), shape((slots, slice_width), BF16)),
        (arrived,),
        flops=GF,
        traffic=MIB // 2,
    )
    pre_parts = call(
        forward_kernel,
        shape((2, slots, hidden_units), F32),
        (rows_x, gate_weight, up_weight),
        flops=GU,
        traffic=MIB // 8,
    )
    own, *parts = call(
        functools.partial(backward_kernel, dp),
        (shape((3, slots, block), F32),) + (shape((3, slots, block), BF16),) * (dp - 1),
        (rows_dy, pre_parts, down_weight),
        scratch=[pltpu.VMEM((slots, hidden_units), F32)],
        flops=5 * 10**8,
        traffic=MIB // 8,
    )
    sums = [own, *[swap(parts[k - 1], k) for k in turns(dp, RS)]]
    turned = call(
        turn_kernel,
        (shape((hidden_units, slice_width), BF16),) * 2,
        (gate_weight, up_weight),
        traffic=4 * MIB,
    )
    own, *turned = lax.optimization_barrier((own, *turned))
    sums[0] = own
    share = call(
        share_kernel,
        shape((3, slots, block), BF16),
        sums,
        traffic=MIB,
    )
    shares = [swap(share, k) for k in turns(dp, AG)]
    results, hidden = call(
        functools.partial(result_kernel, dp),
        (shape((sources, LINES, width), BF16), shape((slots, hidden_units), BF16)),
        (share, *shares, *turned, down_weight),
        scratch=[pltpu.VMEM((2, slots, hidden_units), BF16)],
        flops=6 * cube,
        traffic=8 * MIB,
    )
    back = lax.all_to_all(results, ("expert", "dp"), split_axis=0, concat_axis=0, tiled=True)

    strip = hidden_units // 8
    moments = pl.BlockSpec((1, strip, slice_width), lambda i: (0, i, 0))
    adam = pl.pallas_call(
        adam_kernel,
        grid=(hidden_units // strip,),
        in_specs=[
            SMEM,
            pl.BlockSpec((slots, strip), lambda i: (0, i)),
            pl.BlockSpec((slots, slice_width), lambda i: (0, 0)),
            moments,
            moments,
        ],
        out_specs=(moments, moments, moments),
        out_shape=(shape(first_moment.shape, BF16),) * 3,
        compiler_params=pltpu.CompilerParams(vmem_limit_bytes=32 * MIB),
        cost_estimate=pl.CostEstimate(
            flops=2 * cube, bytes_accessed=10 * MIB, transcendentals=hidden_units * slice_width
        ),
    )(selected, hidden, rows_dy, first_moment, second_moment)

    mixed, input_grad = call(
        functools.partial(combine_kernel, experts, dp),
        (shape((tok_rows, model), BF16), shape((tok_rows, model), BF16)),
        (ones, gates, back),
        out_specs=(own_specs[0],) * 2,
        scratch=[
            pltpu.VMEM((tok_rows, model), BF16),
            pltpu.VMEM((tok_rows, model), BF16),
            pltpu.SemaphoreType.DMA((2, dp)),
        ],
        traffic=4 * MIB,
    )
    return (mixed, input_grad, *adam)


def solution(mesh):
    placed = (
        P(("groups", "expert", "dp"), None),
        P(("groups", "expert", "dp"), None),
        P(("groups", "expert", "dp"), None),
        P(("groups", "expert", "dp"), None),
        P("expert", "dp", None),
        P("expert", "dp", None),
        P("expert", None, "dp"),
        P(("groups", "expert"), None, "dp"),
        P(("groups", "expert"), None, "dp"),
        P("groups"),
    )
    return jax.shard_map(
        local,
        mesh=mesh,
        in_specs=placed,
        out_specs=(
            P(("groups", "expert", "dp"), None),
            P(("groups", "expert", "dp"), None),
            P(("groups", "expert"), None, "dp"),
            P(("groups", "expert"), None, "dp"),
            P(("groups", "expert"), None, "dp"),
        ),
        check_vma=False,
    )
```

```python
import functools

import jax
import jax.numpy as jnp
from jax import lax
from jax.experimental import pallas as pl
from jax.experimental.pallas import tpu as pltpu
from jax.sharding import PartitionSpec as P

CAP = 6
CHUNKS = 4
GROUP = 8
LINES = 2 * CHUNKS * CAP
HALF = CHUNKS * CAP

BETA_ONE = 0.9
BETA_TWO = 0.95
ADAM_EPS = 1e-08

F32 = jnp.float32
BF16 = jnp.bfloat16
VMEM = pl.BlockSpec(memory_space=pltpu.VMEM)
SMEM = pl.BlockSpec(memory_space=pltpu.SMEM)
MIB = 1 << 20
RS = (3, 2, 1)
AG = (2, 1, 3)
MOST = 58
GF = 5 * 10**8
GU = 3 * 10**8


def turns(dp, order):
    return order if dp == len(order) + 1 else tuple(range(1, dp))


def iota(shape, dim):
    return lax.broadcasted_iota(jnp.int32, shape, dim)


def dot(a, b, contract=((1,), (0,))):
    return lax.dot_general(a, b, (contract, ((), ())), preferred_element_type=F32)


def onehot(vector, size, dim):
    return (iota(size, dim) == vector).astype(F32).astype(BF16)


def gather_rows(arrived_ref, targets):
    sources, _, width = arrived_ref.shape
    per, size = GROUP * CAP, GROUP * LINES
    line = iota((1, size), 1)
    source, rest = line // LINES, line % LINES
    order = onehot(rest // CAP * per + source * CAP + rest % CAP, (size, size), 0)
    for g in range(sources // GROUP):
        lines = jnp.concatenate([arrived_ref[g * GROUP + i] for i in range(GROUP)], axis=0)
        sorted_lines = dot(order, lines).astype(BF16)
        for half, target in enumerate(targets):
            for c in range(CHUNKS):
                start = (half * CHUNKS + c) * per
                target[g * per : (g + 1) * per, c * width : (c + 1) * width] = sorted_lines[
                    start : start + per
                ]


def scatter_rows(values, sent_ref):
    sources, _, width = sent_ref.shape
    per, size = GROUP * CAP, GROUP * LINES
    row = iota((1, size), 1)
    part, rest = row // per, row % per
    order = onehot(rest // CAP * LINES + part * CAP + rest % CAP, (size, size), 0)
    for g in range(sources // GROUP):
        lines = jnp.concatenate(
            [
                value[g * per : (g + 1) * per, c * width : (c + 1) * width]
                for value in values
                for c in range(CHUNKS)
            ],
            axis=0,
        )
        sorted_lines = dot(order, lines).astype(BF16)
        for i in range(GROUP):
            sent_ref[g * GROUP + i] = sorted_lines[i * LINES : (i + 1) * LINES]


def dispatch_kernel(
    experts, dp, ids_hbm, codes_hbm, tok_hbm, cot_hbm, sent_ref, ones_ref, gates_ref,
    ids_ref, codes_ref, tok_ref, cot_ref, sems,
):
    copies = [
        pltpu.make_async_copy(a, b, sems.at[i])
        for i, (a, b) in enumerate(
            (
                (ids_hbm, ids_ref),
                (codes_hbm, codes_ref),
                (tok_hbm, tok_ref),
                (cot_hbm, cot_ref),
            )
        )
    ]
    for c in copies:
        c.start()
    rows = tok_ref.shape[0]
    width = tok_ref.shape[1] // dp // CHUNKS
    earlier = (iota((rows, rows), 0) < iota((rows, rows), 1)).astype(F32).astype(BF16)
    copies[0].wait()
    copies[1].wait()
    codes = codes_ref[...].astype(F32)
    gates = (2.5 * codes / jnp.sum(codes, axis=0, keepdims=True)).astype(BF16).astype(F32)
    ids = ids_ref[...]
    matched = [ids == e for e in range(experts)]
    counts = jnp.concatenate(
        [jnp.sum(m.astype(F32), axis=0, keepdims=True) for m in matched], axis=0
    )
    gate_each = [jnp.sum(jnp.where(m, gates, 0.0), axis=0, keepdims=True) for m in matched]
    before = dot(counts.astype(BF16), earlier)
    slot8 = iota((8, rows), 0).astype(F32)
    line = iota((HALF, rows), 0)
    slot_of, chunk_of = (line % CAP).astype(F32), line // CAP
    x_rows, dy_rows = [], []
    for e in range(experts):
        taken = counts[e : e + 1] > 0
        at8 = taken & (before[e : e + 1] == slot8)
        ones_ref[e * 8 : e * 8 + 8, :] = at8.astype(F32)
        gates_ref[e * 8 : e * 8 + 8, :] = jnp.where(at8, gate_each[e], 0.0)
        at = taken & (before[e : e + 1] == slot_of)
        x_rows.append(
            jnp.concatenate([(at & (chunk_of == c)).astype(F32) for c in range(CHUNKS)], axis=1)
        )
        dy_rows.append(
            jnp.concatenate(
                [jnp.where(at & (chunk_of == c), gate_each[e], 0.0) for c in range(CHUNKS)], axis=1
            )
        )
    x_rows = jnp.concatenate(x_rows, axis=0).astype(BF16)
    dy_rows = jnp.concatenate(dy_rows, axis=0).astype(BF16)
    for copy, source_ref, weights, half in (
        (copies[2], tok_ref, x_rows, 0),
        (copies[3], cot_ref, dy_rows, HALF),
    ):
        copy.wait()
        for j in range(dp):
            base = j * width * CHUNKS
            lines = jnp.concatenate(
                [
                    source_ref[:, base + c * width : base + (c + 1) * width]
                    for c in range(CHUNKS)
                ],
                axis=0,
            )
            out = dot(weights, lines)
            for e in range(experts):
                sent_ref[e * dp + j, half : half + HALF] = out[
                    e * HALF : (e + 1) * HALF
                ].astype(BF16)


def gather_kernel(arrived_ref, rows_x, rows_dy):
    gather_rows(arrived_ref, (rows_x, rows_dy))


def forward_kernel(rows_x, gate_w, up_w, total):
    total[0] = dot(rows_x[...], gate_w[0])
    total[1] = dot(rows_x[...], up_w[0])


def backward_kernel(dp, rows_dy, pre_ref, down_w, own_ref, *refs):
    sent, (total,) = refs[: dp - 1], refs[dp - 1 :]
    total[...] = dot(rows_dy[...], down_w[0], ((1,), (1,)))
    me = lax.axis_index("dp")
    block = total.shape[1] // dp
    for k in range(dp):
        at = pl.ds(pl.multiple_of(jnp.bitwise_xor(me, k) * block, block), block)
        target = own_ref if k == 0 else sent[k - 1]
        target[:2] = pre_ref[:, :, at].astype(target.dtype)
        target[2] = total[:, at].astype(target.dtype)


def summed(refs, i):
    return sum([r[i].astype(F32) for r in refs[1:]], refs[0][i])


def share_kernel(*refs):
    sums, share_ref = refs[:-1], refs[-1]
    gate, up, grad = [summed(sums, i) for i in range(3)]
    sig = jax.nn.sigmoid(gate)
    share_ref[0] = (gate * sig * up).astype(BF16)
    share_ref[1] = (grad * up * sig * (1.0 + gate * (1.0 - sig))).astype(BF16)
    share_ref[2] = (grad * gate * sig).astype(BF16)


def turn_kernel(*refs):
    count = len(refs) // 2
    for source, target in zip(refs[:count], refs[count:]):
        target[...] = source[0].T


def result_kernel(dp, *refs):
    arrived = refs[:dp]
    order = (0, *turns(dp, AG))
    gate_w, up_w, down_w, sent_ref, hidden_ref, full = refs[dp:]
    me = lax.axis_index("dp")
    block = arrived[0].shape[2]
    for i, k in enumerate(order):
        at = pl.multiple_of(jnp.bitwise_xor(me, k) * block, block)
        hidden_ref[:, pl.ds(at, block)] = arrived[i][0]
        full[:, :, pl.ds(at, block)] = arrived[i][1:]
    out = dot(hidden_ref[...], down_w[0])
    grad = dot(full[0], gate_w[...]) + dot(full[1], up_w[...])
    scatter_rows((out.astype(BF16), grad.astype(BF16)), sent_ref)


def adam_kernel(selected_ref, hidden_ref, dy_ref, first_ref, second_ref, step_ref, one_ref, two_ref):
    me = lax.axis_index("expert")
    chosen = selected_ref[0] == me
    for i in range(1, selected_ref.shape[0]):
        chosen = chosen | (selected_ref[i] == me)

    @pl.when(chosen)
    def _():
        grad = dot(hidden_ref[...], dy_ref[...], ((0,), (0,)))
        one = BETA_ONE * first_ref[0].astype(F32) + (1.0 - BETA_ONE) * grad
        two = BETA_TWO * second_ref[0].astype(F32) + (1.0 - BETA_TWO) * grad * grad
        step_ref[0] = (one / (jnp.sqrt(two) + ADAM_EPS)).astype(BF16)
        one_ref[0] = one.astype(BF16)
        two_ref[0] = two.astype(BF16)

    @pl.when(jnp.logical_not(chosen))
    def _():
        step_ref[...] = jnp.zeros_like(step_ref)
        one_ref[...] = first_ref[...]
        two_ref[...] = second_ref[...]


def spread_kernel(experts, ones_ref, gates_ref, spread_ref):
    small = (experts * 8, experts * LINES)
    source, target = iota(small, 0), iota(small, 1)
    same = (source // 8 == target // LINES) & (source % 8 < CAP)
    within = target % LINES - source % 8
    for half, ref in enumerate((gates_ref, ones_ref)):
        weights = ref[...].astype(BF16)
        for c in range(CHUNKS):
            spot = same & (within == half * HALF + c * CAP)
            spread = dot(weights, spot.astype(F32).astype(BF16), ((0,), (0,)))
            spread_ref[half * CHUNKS + c] = spread.astype(BF16)


def combine_kernel(experts, dp, spread_ref, back_ref, mixed_hbm, grad_hbm, mixed_ref, grad_ref, sems):
    width = back_ref.shape[2]
    copies = []
    for j in range(dp):
        lines = jnp.concatenate([back_ref[e * dp + j] for e in range(experts)], axis=0)
        for half, ref, hbm in ((0, mixed_ref, mixed_hbm), (1, grad_ref, grad_hbm)):
            for c in range(CHUNKS):
                at = (j * CHUNKS + c) * width
                ref[:, at : at + width] = dot(spread_ref[half * CHUNKS + c], lines).astype(BF16)
            span = pl.ds(j * CHUNKS * width, CHUNKS * width)
            copies.append(pltpu.make_async_copy(ref.at[:, span], hbm.at[:, span], sems.at[half, j]))
            copies[-1].start()
    for c in copies:
        c.wait()


def call(kernel, outs, operands, in_specs=None, out_specs=None, scratch=(), limit=24, flops=0, traffic=0):
    return pl.pallas_call(
        kernel,
        out_shape=outs,
        in_specs=in_specs or [VMEM] * len(operands),
        out_specs=out_specs or jax.tree.map(lambda _: VMEM, outs),
        scratch_shapes=scratch,
        compiler_params=pltpu.CompilerParams(vmem_limit_bytes=int(limit * MIB)),
        cost_estimate=pl.CostEstimate(flops=flops, bytes_accessed=traffic, transcendentals=0),
    )(*operands)


def local(
    tokens,
    expert_ids,
    gate_codes,
    cotangent,
    gate_weight,
    up_weight,
    down_weight,
    first_moment,
    second_moment,
    selected,
):
    experts = lax.axis_size("expert")
    dp = lax.axis_size("dp")
    tok_rows, model = tokens.shape
    slice_width = model // dp
    width = slice_width // CHUNKS
    hidden_units = gate_weight.shape[2]
    block = hidden_units // dp
    sources = experts * dp
    slots = sources * CAP
    shape = jax.ShapeDtypeStruct
    cube = slots * slice_width * hidden_units
    own_specs = [pl.BlockSpec(memory_space=pltpu.HBM)] * 4

    sent, ones, gates = call(
        functools.partial(dispatch_kernel, experts, dp),
        (
            shape((sources, LINES, width), BF16),
            shape((experts * 8, tok_rows), F32),
            shape((experts * 8, tok_rows), F32),
        ),
        (expert_ids.T, gate_codes.T, tokens, cotangent),
        in_specs=own_specs,
        limit=MOST,
        scratch=[
            pltpu.VMEM(expert_ids.shape[::-1], jnp.int32),
            pltpu.VMEM(gate_codes.shape[::-1], jnp.int32),
            pltpu.VMEM(tokens.shape, BF16),
            pltpu.VMEM(cotangent.shape, BF16),
            pltpu.SemaphoreType.DMA((4,)),
        ],
        traffic=6 * MIB,
    )
    arrived = lax.all_to_all(sent, ("expert", "dp"), split_axis=0, concat_axis=0, tiled=True)
    def swap(value, k):
        return lax.ppermute(value, "dp", [(i, i ^ k) for i in range(dp)])

    def swaps(values):
        return [swap(values[k - 1], k) for k in range(1, dp)]

    weights = (gate_weight, up_weight, down_weight)

    rows_x, rows_dy = call(
        gather_kernel,
        (shape((slots, slice_width), BF16), shape((slots, slice_width), BF16)),
        (arrived,),
        flops=GF,
        traffic=MIB // 2,
    )
    pre_parts = call(
        forward_kernel,
        shape((2, slots, hidden_units), F32),
        (rows_x, gate_weight, up_weight),
        flops=GU,
        traffic=MIB // 8,
    )
    own, *parts = call(
        functools.partial(backward_kernel, dp),
        (shape((3, slots, block), F32),) + (shape((3, slots, block), BF16),) * (dp - 1),
        (rows_dy, pre_parts, down_weight),
        scratch=[pltpu.VMEM((slots, hidden_units), F32)],
        flops=5 * 10**8,
        traffic=MIB // 8,
    )
    sums = [own, *[swap(parts[k - 1], k) for k in turns(dp, RS)]]
    turned = call(
        turn_kernel,
        (shape((hidden_units, slice_width), BF16),) * 2,
        (gate_weight, up_weight),
        traffic=4 * MIB,
    )
    spread = call(
        functools.partial(spread_kernel, experts),
        shape((2 * CHUNKS, tok_rows, experts * LINES), BF16),
        (ones, gates),
        traffic=MIB // 2,
    )
    own, spread, *turned = lax.optimization_barrier((own, spread, *turned))
    sums[0] = own
    share = call(
        share_kernel,
        shape((3, slots, block), BF16),
        sums,
        traffic=MIB,
    )
    shares = [swap(share, k) for k in turns(dp, AG)]
    results, hidden = call(
        functools.partial(result_kernel, dp),
        (shape((sources, LINES, width), BF16), shape((slots, hidden_units), BF16)),
        (share, *shares, *turned, down_weight),
        scratch=[pltpu.VMEM((2, slots, hidden_units), BF16)],
        flops=6 * cube,
        traffic=8 * MIB,
    )
    back = lax.all_to_all(results, ("expert", "dp"), split_axis=0, concat_axis=0, tiled=True)

    strip = hidden_units // 8
    moments = pl.BlockSpec((1, strip, slice_width), lambda i: (0, i, 0))
    adam = pl.pallas_call(
        adam_kernel,
        grid=(hidden_units // strip,),
        in_specs=[
            SMEM,
            pl.BlockSpec((slots, strip), lambda i: (0, i)),
            pl.BlockSpec((slots, slice_width), lambda i: (0, 0)),
            moments,
            moments,
        ],
        out_specs=(moments, moments, moments),
        out_shape=(shape(first_moment.shape, BF16),) * 3,
        compiler_params=pltpu.CompilerParams(vmem_limit_bytes=32 * MIB),
        cost_estimate=pl.CostEstimate(
            flops=2 * cube, bytes_accessed=10 * MIB, transcendentals=hidden_units * slice_width
        ),
    )(selected, hidden, rows_dy, first_moment, second_moment)

    mixed, input_grad = call(
        functools.partial(combine_kernel, experts, dp),
        (shape((tok_rows, model), BF16), shape((tok_rows, model), BF16)),
        (spread, back),
        out_specs=(own_specs[0],) * 2,
        scratch=[
            pltpu.VMEM((tok_rows, model), BF16),
            pltpu.VMEM((tok_rows, model), BF16),
            pltpu.SemaphoreType.DMA((2, dp)),
        ],
        traffic=4 * MIB,
    )
    return (mixed, input_grad, *adam)


def solution(mesh):
    placed = (
        P(("groups", "expert", "dp"), None),
        P(("groups", "expert", "dp"), None),
        P(("groups", "expert", "dp"), None),
        P(("groups", "expert", "dp"), None),
        P("expert", "dp", None),
        P("expert", "dp", None),
        P("expert", None, "dp"),
        P(("groups", "expert"), None, "dp"),
        P(("groups", "expert"), None, "dp"),
        P("groups"),
    )
    return jax.shard_map(
        local,
        mesh=mesh,
        in_specs=placed,
        out_specs=(
            P(("groups", "expert", "dp"), None),
            P(("groups", "expert", "dp"), None),
            P(("groups", "expert"), None, "dp"),
            P(("groups", "expert"), None, "dp"),
            P(("groups", "expert"), None, "dp"),
        ),
        check_vma=False,
    )
```

```python
import functools

import jax
import jax.numpy as jnp
from jax import lax
from jax.experimental import pallas as pl
from jax.experimental.pallas import tpu as pltpu
from jax.sharding import PartitionSpec as P

CAP = 6
CHUNKS = 4
GROUP = 4
LINES = 2 * CHUNKS * CAP
HALF = CHUNKS * CAP

BETA_ONE = 0.9
BETA_TWO = 0.95
ADAM_EPS = 1e-08

F32 = jnp.float32
BF16 = jnp.bfloat16
VMEM = pl.BlockSpec(memory_space=pltpu.VMEM)
SMEM = pl.BlockSpec(memory_space=pltpu.SMEM)
MIB = 1 << 20
RS = (3, 2, 1)
AG = (2, 1, 3)
MOST = 58
GF = 5 * 10**8
GU = 3 * 10**8


def turns(dp, order):
    return order if dp == len(order) + 1 else tuple(range(1, dp))


def iota(shape, dim):
    return lax.broadcasted_iota(jnp.int32, shape, dim)


def dot(a, b, contract=((1,), (0,))):
    return lax.dot_general(a, b, (contract, ((), ())), preferred_element_type=F32)


def onehot(vector, size, dim):
    return (iota(size, dim) == vector).astype(F32).astype(BF16)


def gather_rows(arrived_ref, targets):
    sources, _, width = arrived_ref.shape
    per, size = GROUP * CAP, GROUP * LINES
    line = iota((1, size), 1)
    source, rest = line // LINES, line % LINES
    order = onehot(rest // CAP * per + source * CAP + rest % CAP, (size, size), 0)
    for g in range(sources // GROUP):
        lines = jnp.concatenate([arrived_ref[g * GROUP + i] for i in range(GROUP)], axis=0)
        sorted_lines = dot(order, lines).astype(BF16)
        for half, target in enumerate(targets):
            for c in range(CHUNKS):
                start = (half * CHUNKS + c) * per
                target[g * per : (g + 1) * per, c * width : (c + 1) * width] = sorted_lines[
                    start : start + per
                ]


def scatter_rows(values, sent_ref):
    sources, _, width = sent_ref.shape
    per, size = GROUP * CAP, GROUP * LINES
    row = iota((1, size), 1)
    part, rest = row // per, row % per
    order = onehot(rest // CAP * LINES + part * CAP + rest % CAP, (size, size), 0)
    for g in range(sources // GROUP):
        lines = jnp.concatenate(
            [
                value[g * per : (g + 1) * per, c * width : (c + 1) * width]
                for value in values
                for c in range(CHUNKS)
            ],
            axis=0,
        )
        sorted_lines = dot(order, lines).astype(BF16)
        for i in range(GROUP):
            sent_ref[g * GROUP + i] = sorted_lines[i * LINES : (i + 1) * LINES]


def dispatch_kernel(
    experts, dp, ids_hbm, codes_hbm, tok_hbm, cot_hbm, sent_ref, ones_ref, gates_ref,
    ids_ref, codes_ref, tok_ref, cot_ref, sems,
):
    copies = [
        pltpu.make_async_copy(a, b, sems.at[i])
        for i, (a, b) in enumerate(
            (
                (ids_hbm, ids_ref),
                (codes_hbm, codes_ref),
                (tok_hbm, tok_ref),
                (cot_hbm, cot_ref),
            )
        )
    ]
    for c in copies:
        c.start()
    rows = tok_ref.shape[0]
    width = tok_ref.shape[1] // dp // CHUNKS
    earlier = (iota((rows, rows), 0) < iota((rows, rows), 1)).astype(F32).astype(BF16)
    copies[0].wait()
    copies[1].wait()
    codes = codes_ref[...].astype(F32)
    gates = (2.5 * codes / jnp.sum(codes, axis=0, keepdims=True)).astype(BF16).astype(F32)
    ids = ids_ref[...]
    matched = [ids == e for e in range(experts)]
    counts = jnp.concatenate(
        [jnp.sum(m.astype(F32), axis=0, keepdims=True) for m in matched], axis=0
    )
    gate_each = [jnp.sum(jnp.where(m, gates, 0.0), axis=0, keepdims=True) for m in matched]
    before = dot(counts.astype(BF16), earlier)
    slot8 = iota((8, rows), 0).astype(F32)
    line = iota((HALF, rows), 0)
    slot_of, chunk_of = (line % CAP).astype(F32), line // CAP
    x_rows, dy_rows = [], []
    for e in range(experts):
        taken = counts[e : e + 1] > 0
        at8 = taken & (before[e : e + 1] == slot8)
        ones_ref[e * 8 : e * 8 + 8, :] = at8.astype(F32)
        gates_ref[e * 8 : e * 8 + 8, :] = jnp.where(at8, gate_each[e], 0.0)
        at = taken & (before[e : e + 1] == slot_of)
        x_rows.append(
            jnp.concatenate([(at & (chunk_of == c)).astype(F32) for c in range(CHUNKS)], axis=1)
        )
        dy_rows.append(
            jnp.concatenate(
                [jnp.where(at & (chunk_of == c), gate_each[e], 0.0) for c in range(CHUNKS)], axis=1
            )
        )
    x_rows = jnp.concatenate(x_rows, axis=0).astype(BF16)
    dy_rows = jnp.concatenate(dy_rows, axis=0).astype(BF16)
    for copy, source_ref, weights, half in (
        (copies[2], tok_ref, x_rows, 0),
        (copies[3], cot_ref, dy_rows, HALF),
    ):
        copy.wait()
        for j in range(dp):
            base = j * width * CHUNKS
            lines = jnp.concatenate(
                [
                    source_ref[:, base + c * width : base + (c + 1) * width]
                    for c in range(CHUNKS)
                ],
                axis=0,
            )
            out = dot(weights, lines)
            for e in range(experts):
                sent_ref[e * dp + j, half : half + HALF] = out[
                    e * HALF : (e + 1) * HALF
                ].astype(BF16)


def gather_kernel(arrived_ref, rows_x, rows_dy):
    gather_rows(arrived_ref, (rows_x, rows_dy))


def forward_kernel(rows_x, gate_w, up_w, total):
    total[0] = dot(rows_x[...], gate_w[0])
    total[1] = dot(rows_x[...], up_w[0])


def backward_kernel(dp, rows_dy, pre_ref, down_w, own_ref, *refs):
    sent, (total,) = refs[: dp - 1], refs[dp - 1 :]
    total[...] = dot(rows_dy[...], down_w[0], ((1,), (1,)))
    me = lax.axis_index("dp")
    block = total.shape[1] // dp
    for k in range(dp):
        at = pl.ds(pl.multiple_of(jnp.bitwise_xor(me, k) * block, block), block)
        target = own_ref if k == 0 else sent[k - 1]
        target[:2] = pre_ref[:, :, at].astype(target.dtype)
        target[2] = total[:, at].astype(target.dtype)


def summed(refs, i):
    return sum([r[i].astype(F32) for r in refs[1:]], refs[0][i])


def share_kernel(*refs):
    sums, share_ref = refs[:-1], refs[-1]
    gate, up, grad = [summed(sums, i) for i in range(3)]
    sig = jax.nn.sigmoid(gate)
    share_ref[0] = (gate * sig * up).astype(BF16)
    share_ref[1] = (grad * up * sig * (1.0 + gate * (1.0 - sig))).astype(BF16)
    share_ref[2] = (grad * gate * sig).astype(BF16)


def turn_kernel(*refs):
    count = len(refs) // 2
    for source, target in zip(refs[:count], refs[count:]):
        target[...] = source[0].T


def result_kernel(dp, *refs):
    arrived = refs[:dp]
    order = (0, *turns(dp, AG))
    gate_w, up_w, down_w, sent_ref, hidden_ref, full = refs[dp:]
    me = lax.axis_index("dp")
    block = arrived[0].shape[2]
    for i, k in enumerate(order):
        at = pl.multiple_of(jnp.bitwise_xor(me, k) * block, block)
        hidden_ref[:, pl.ds(at, block)] = arrived[i][0]
        full[:, :, pl.ds(at, block)] = arrived[i][1:]
    out = dot(hidden_ref[...], down_w[0])
    grad = dot(full[0], gate_w[...]) + dot(full[1], up_w[...])
    scatter_rows((out.astype(BF16), grad.astype(BF16)), sent_ref)


def adam_kernel(selected_ref, hidden_ref, dy_ref, first_ref, second_ref, step_ref, one_ref, two_ref):
    me = lax.axis_index("expert")
    chosen = selected_ref[0] == me
    for i in range(1, selected_ref.shape[0]):
        chosen = chosen | (selected_ref[i] == me)

    @pl.when(chosen)
    def _():
        grad = dot(hidden_ref[...], dy_ref[...], ((0,), (0,)))
        one = BETA_ONE * first_ref[0].astype(F32) + (1.0 - BETA_ONE) * grad
        two = BETA_TWO * second_ref[0].astype(F32) + (1.0 - BETA_TWO) * grad * grad
        step_ref[0] = (one / (jnp.sqrt(two) + ADAM_EPS)).astype(BF16)
        one_ref[0] = one.astype(BF16)
        two_ref[0] = two.astype(BF16)

    @pl.when(jnp.logical_not(chosen))
    def _():
        step_ref[...] = jnp.zeros_like(step_ref)
        one_ref[...] = first_ref[...]
        two_ref[...] = second_ref[...]


def spread_kernel(experts, ones_ref, gates_ref, spread_ref):
    small = (experts * 8, experts * LINES)
    source, target = iota(small, 0), iota(small, 1)
    same = (source // 8 == target // LINES) & (source % 8 < CAP)
    within = target % LINES - source % 8
    for half, ref in enumerate((gates_ref, ones_ref)):
        weights = ref[...].astype(BF16)
        for c in range(CHUNKS):
            spot = same & (within == half * HALF + c * CAP)
            spread = dot(weights, spot.astype(F32).astype(BF16), ((0,), (0,)))
            spread_ref[half * CHUNKS + c] = spread.astype(BF16)


def combine_kernel(experts, dp, spread_ref, back_ref, mixed_hbm, grad_hbm, mixed_ref, grad_ref, sems):
    width = back_ref.shape[2]
    copies = []
    for j in range(dp):
        lines = jnp.concatenate([back_ref[e * dp + j] for e in range(experts)], axis=0)
        for half, ref, hbm in ((0, mixed_ref, mixed_hbm), (1, grad_ref, grad_hbm)):
            for c in range(CHUNKS):
                at = (j * CHUNKS + c) * width
                ref[:, at : at + width] = dot(spread_ref[half * CHUNKS + c], lines).astype(BF16)
            span = pl.ds(j * CHUNKS * width, CHUNKS * width)
            copies.append(pltpu.make_async_copy(ref.at[:, span], hbm.at[:, span], sems.at[half, j]))
            copies[-1].start()
    for c in copies:
        c.wait()


def call(kernel, outs, operands, in_specs=None, out_specs=None, scratch=(), limit=24, flops=0, traffic=0):
    return pl.pallas_call(
        kernel,
        out_shape=outs,
        in_specs=in_specs or [VMEM] * len(operands),
        out_specs=out_specs or jax.tree.map(lambda _: VMEM, outs),
        scratch_shapes=scratch,
        compiler_params=pltpu.CompilerParams(vmem_limit_bytes=int(limit * MIB)),
        cost_estimate=pl.CostEstimate(flops=flops, bytes_accessed=traffic, transcendentals=0),
    )(*operands)


def local(
    tokens,
    expert_ids,
    gate_codes,
    cotangent,
    gate_weight,
    up_weight,
    down_weight,
    first_moment,
    second_moment,
    selected,
):
    experts = lax.axis_size("expert")
    dp = lax.axis_size("dp")
    tok_rows, model = tokens.shape
    slice_width = model // dp
    width = slice_width // CHUNKS
    hidden_units = gate_weight.shape[2]
    block = hidden_units // dp
    sources = experts * dp
    slots = sources * CAP
    shape = jax.ShapeDtypeStruct
    cube = slots * slice_width * hidden_units
    own_specs = [pl.BlockSpec(memory_space=pltpu.HBM)] * 4

    sent, ones, gates = call(
        functools.partial(dispatch_kernel, experts, dp),
        (
            shape((sources, LINES, width), BF16),
            shape((experts * 8, tok_rows), F32),
            shape((experts * 8, tok_rows), F32),
        ),
        (expert_ids.T, gate_codes.T, tokens, cotangent),
        in_specs=own_specs,
        limit=MOST,
        scratch=[
            pltpu.VMEM(expert_ids.shape[::-1], jnp.int32),
            pltpu.VMEM(gate_codes.shape[::-1], jnp.int32),
            pltpu.VMEM(tokens.shape, BF16),
            pltpu.VMEM(cotangent.shape, BF16),
            pltpu.SemaphoreType.DMA((4,)),
        ],
        traffic=6 * MIB,
    )
    arrived = lax.all_to_all(sent, ("expert", "dp"), split_axis=0, concat_axis=0, tiled=True)
    def swap(value, k):
        return lax.ppermute(value, "dp", [(i, i ^ k) for i in range(dp)])

    def swaps(values):
        return [swap(values[k - 1], k) for k in range(1, dp)]

    weights = (gate_weight, up_weight, down_weight)

    rows_x, rows_dy = call(
        gather_kernel,
        (shape((slots, slice_width), BF16), shape((slots, slice_width), BF16)),
        (arrived,),
        flops=GF,
        traffic=MIB // 2,
    )
    pre_parts = call(
        forward_kernel,
        shape((2, slots, hidden_units), F32),
        (rows_x, gate_weight, up_weight),
        flops=GU,
        traffic=MIB // 8,
    )
    own, *parts = call(
        functools.partial(backward_kernel, dp),
        (shape((3, slots, block), F32),) + (shape((3, slots, block), BF16),) * (dp - 1),
        (rows_dy, pre_parts, down_weight),
        scratch=[pltpu.VMEM((slots, hidden_units), F32)],
        flops=5 * 10**8,
        traffic=MIB // 8,
    )
    sums = [own, *[swap(parts[k - 1], k) for k in turns(dp, RS)]]
    turned = call(
        turn_kernel,
        (shape((hidden_units, slice_width), BF16),) * 2,
        (gate_weight, up_weight),
        traffic=4 * MIB,
    )
    spread = call(
        functools.partial(spread_kernel, experts),
        shape((2 * CHUNKS, tok_rows, experts * LINES), BF16),
        (ones, gates),
        traffic=MIB // 2,
    )
    own, spread, *turned = lax.optimization_barrier((own, spread, *turned))
    sums[0] = own
    share = call(
        share_kernel,
        shape((3, slots, block), BF16),
        sums,
        traffic=MIB,
    )
    shares = [swap(share, k) for k in turns(dp, AG)]
    results, hidden = call(
        functools.partial(result_kernel, dp),
        (shape((sources, LINES, width), BF16), shape((slots, hidden_units), BF16)),
        (share, *shares, *turned, down_weight),
        scratch=[pltpu.VMEM((2, slots, hidden_units), BF16)],
        flops=6 * cube,
        traffic=8 * MIB,
    )
    back = lax.all_to_all(results, ("expert", "dp"), split_axis=0, concat_axis=0, tiled=True)

    strip = hidden_units // 8
    moments = pl.BlockSpec((1, strip, slice_width), lambda i: (0, i, 0))
    adam = pl.pallas_call(
        adam_kernel,
        grid=(hidden_units // strip,),
        in_specs=[
            SMEM,
            pl.BlockSpec((slots, strip), lambda i: (0, i)),
            pl.BlockSpec((slots, slice_width), lambda i: (0, 0)),
            moments,
            moments,
        ],
        out_specs=(moments, moments, moments),
        out_shape=(shape(first_moment.shape, BF16),) * 3,
        compiler_params=pltpu.CompilerParams(vmem_limit_bytes=32 * MIB),
        cost_estimate=pl.CostEstimate(
            flops=2 * cube, bytes_accessed=10 * MIB, transcendentals=hidden_units * slice_width
        ),
    )(selected, hidden, rows_dy, first_moment, second_moment)

    mixed, input_grad = call(
        functools.partial(combine_kernel, experts, dp),
        (shape((tok_rows, model), BF16), shape((tok_rows, model), BF16)),
        (spread, back),
        out_specs=(own_specs[0],) * 2,
        scratch=[
            pltpu.VMEM((tok_rows, model), BF16),
            pltpu.VMEM((tok_rows, model), BF16),
            pltpu.SemaphoreType.DMA((2, dp)),
        ],
        traffic=4 * MIB,
    )
    return (mixed, input_grad, *adam)


def solution(mesh):
    placed = (
        P(("groups", "expert", "dp"), None),
        P(("groups", "expert", "dp"), None),
        P(("groups", "expert", "dp"), None),
        P(("groups", "expert", "dp"), None),
        P("expert", "dp", None),
        P("expert", "dp", None),
        P("expert", None, "dp"),
        P(("groups", "expert"), None, "dp"),
        P(("groups", "expert"), None, "dp"),
        P("groups"),
    )
    return jax.shard_map(
        local,
        mesh=mesh,
        in_specs=placed,
        out_specs=(
            P(("groups", "expert", "dp"), None),
            P(("groups", "expert", "dp"), None),
            P(("groups", "expert"), None, "dp"),
            P(("groups", "expert"), None, "dp"),
            P(("groups", "expert"), None, "dp"),
        ),
        check_vma=False,
    )
```
